32 devices in a mesh: view: 8 (over y, x, core), bulk: 4 (over z).
Axes of the slice: x: 2, y: 2, z: 4, core: 2. Of those that a mesh axis runs over, the one named last changes fastest.
Arguments:
- estimate: float32 [128, 32, 128], P('bulk'), may hold values from 0.5 to 2
- image: float32 [8, 128, 32, 128], P('view', 'bulk'), may hold values from 0.05 to 20, as said below
- psf: float32 [8, 3, 15], P('view'), may hold values from 0.05 to 1
- perm: int32 [8], P('view'), may hold values from 0 to 1
- shift: int32 [8], P('view'), may hold values from -8 to 7
- visible: int32 [8, 128], P('view', 'bulk'), may hold values 0 or 1
Outputs:
- updated: float32 [128, 32, 128], P('bulk')
The draws below stay inside these ranges and needn't reach their ends.
Inputs may be any that keep to these rules, and one draw needn't show every extreme that they name: `image`: every entry is positive.
All inputs are finite; a program needn't handle non-finite values. No bound on the sum of `visible` on one device may be relied on, other than what follows from the above.
Results may differ from the reference program's by a relative error of at most 0.0003.
Values sent between devices are 32-bit elements; how exact they have to be, the bound alone decides.
No kernel may reach another device: no remote copies, remote signals or barrier semaphores. Data moves between devices by JAX's collectives and lax.ppermute only.
A program may use at most 128 MiB of HBM per device.

```python
import math
import jax
import jax.numpy as jnp
from jax import lax

NY = 32
TAPS = 15
VIEWS = 8
NZ = 128
NX = 128


def draw_image(key, part):
    rough_key, size_key, sign_key, phase_key = jax.random.split(key, 4)
    shape = (VIEWS, NZ, NY, NX)
    rough = jnp.exp(jax.random.uniform(rough_key, shape, jnp.float32, math.log(0.5), math.log(2.0)))
    amplitude = 0.45
    magnitude = jax.random.uniform(size_key, (VIEWS, 4, 3), jnp.float32, 1.0 / 64.0, 1.0 / 24.0)
    signs = jnp.where(jax.random.bernoulli(sign_key, 0.5, (VIEWS, 4, 3)), 1.0, -1.0).astype(jnp.float32)
    freqs = magnitude * signs
    phases = jax.random.uniform(phase_key, (VIEWS, 4), jnp.float32, 0.0, 1.0)
    zpos = jnp.arange(NZ, dtype=jnp.float32)[None, :, None, None]
    ypos = jnp.arange(NY, dtype=jnp.float32)[None, None, :, None]
    xpos = jnp.arange(NX, dtype=jnp.float32)[None, None, None, :]
    field = jnp.zeros(shape, jnp.float32)
    for wave in range(4):
        along_z = jnp.mod(freqs[:, wave, 0][:, None, None, None] * zpos, 1.0)
        along_y = jnp.mod(freqs[:, wave, 1][:, None, None, None] * ypos, 1.0)
        along_x = jnp.mod(freqs[:, wave, 2][:, None, None, None] * xpos, 1.0)
        cycles = jnp.mod(along_z + along_y + along_x + phases[:, wave][:, None, None, None], 1.0)
        field = field + jnp.cos(2.0 * math.pi * cycles)
    return (rough * jnp.exp(amplitude * field)).astype(jnp.float32)


def with_ends(entries, own_key, low, high):
    longest = entries.shape.index(max(entries.shape))
    spots = []
    for shift in (0, 1):
        where = [jax.random.randint(jax.random.fold_in(own_key, axis), (), 0, length) for axis, length in enumerate(entries.shape)]
        where[longest] = (where[longest] + shift) % entries.shape[longest]
        spots.append(tuple(where))
    return entries.at[spots[0]].set(low).at[spots[1]].set(high)


def block_levels(key, dims, cuts, smallest, top_value):
    def one(dim, shards_of):
        steps = jax.random.uniform(jax.random.fold_in(jax.random.fold_in(key, 6), dim), (shards_of,), jnp.float32, smallest / len(cuts), top_value / len(cuts))
        return jnp.repeat(jnp.exp(steps), dims[dim] // shards_of).reshape((-1,) + (1,) * (len(dims) - dim - 1))

    gain = one(*cuts[0])
    for cut in cuts[1:]:
        gain = gain * one(*cut)
    return gain


def setup_inputs(seed: int = 0) -> dict:
    keys = jax.random.split(jax.random.key(seed), 7)
    return {
        "estimate": jnp.clip(jnp.exp(math.log(2.0) - 1.3862944 * jax.random.uniform(keys[0], (NZ, NY, NX), jnp.float32) ** block_levels(keys[0], (NZ, NY, NX), ((0, 4),), -0.2, 0.2)), 0.5, 2.0),
        "image": draw_image(jax.random.fold_in(keys[6], 71), 0),
        "psf": jnp.clip(jnp.exp(math.log(1.0) - 2.9957323 * jax.random.uniform(keys[2], (VIEWS, 3, TAPS), jnp.float32) ** block_levels(keys[2], (VIEWS, 3, TAPS), ((0, 8),), -0.2, 0.2)), 0.05, 1.0),
        "perm": with_ends(jax.random.randint(keys[3], (VIEWS,), 0, 2), jax.random.fold_in(keys[3], 1), 0, 1).astype(jnp.int32),
        "shift": with_ends(jax.random.randint(keys[4], (VIEWS,), 0 - NY // 4, NY // 4), jax.random.fold_in(keys[4], 1), 0 - NY // 4, (NY // 4) - 1).astype(jnp.int32),
        "visible": with_ends((jax.random.randint(keys[5], (VIEWS, NZ), 0, 3) < 2).astype(jnp.int32), jax.random.fold_in(keys[5], 1), 0, 1),
    }


def blur_axis(values, kernel, axis, cyclic):
    margin = kernel.shape[0] // 2
    widths = [(0, 0)] * values.ndim
    widths[axis] = (margin, margin)
    padded = jnp.pad(values, widths, mode="wrap" if cyclic else "constant")
    extent = values.shape[axis]
    summed = jnp.zeros(values.shape, jnp.float32)
    for offset in range(kernel.shape[0]):
        summed = summed + kernel[offset] * lax.slice_in_dim(padded, offset, offset + extent, axis=axis)
    return summed


def reference(estimate, image, psf, perm, shift, visible):
    def one_view(log_total, inputs):
        stack, raw_taps, turned, moved, seen = inputs
        kernels = raw_taps / jnp.sum(raw_taps, axis=1, keepdims=True)
        framed = jnp.where(turned == 1, jnp.transpose(estimate, (2, 1, 0)), estimate)
        viewed = jnp.roll(framed, moved, axis=1)
        blurred = blur_axis(blur_axis(blur_axis(viewed, kernels[0], 0, False), kernels[1], 1, True), kernels[2], 2, False)
        ratio = stack / blurred
        flipped = kernels[:, ::-1]
        correction = blur_axis(blur_axis(blur_axis(ratio, flipped[2], 2, False), flipped[1], 1, True), flipped[0], 0, False)
        unrolled = jnp.roll(correction, -moved, axis=1)
        joined = jnp.where(turned == 1, jnp.transpose(unrolled, (2, 1, 0)), unrolled)
        weight = jnp.where(seen == 1, 1.0, 0.0).astype(jnp.float32)
        return log_total + weight[:, None, None] * jnp.log(joined), None

    log_total, unused = lax.scan(one_view, jnp.zeros(estimate.shape, jnp.float32), (image, psf, perm, shift, visible))
    return estimate * jnp.exp(log_total / VIEWS)
```

```python
import functools

import jax
import jax.numpy as jnp
from jax import lax
from jax.experimental import pallas as pl
from jax.experimental.pallas import tpu as pltpu
from jax.sharding import PartitionSpec as P

LANES = 128
ROWS = 8
WIDE = 256
VMEM = pl.BlockSpec(memory_space=pltpu.VMEM)
SMEM = pl.BlockSpec(memory_space=pltpu.SMEM)
PARAMS = pltpu.CompilerParams(vmem_limit_bytes=40 * 1024 * 1024)


def struct(shape, dtype=jnp.float32):
    return jax.ShapeDtypeStruct(shape, dtype)


def halves(values):
    high = values.astype(jnp.bfloat16)
    low = (values - high.astype(jnp.float32)).astype(jnp.bfloat16)
    return high, low


def dot(left, right):
    return jnp.dot(left, right, preferred_element_type=jnp.float32)


def blur_rows(left_high, left_low, values):
    width = values.shape[1]
    high, low = halves(values)
    both = dot(left_high, jnp.concatenate([high, low], axis=1))
    return both[:, :width] + both[:, width:] + dot(left_low, high)


def blur_lanes(right, values):
    width = values.shape[1]
    out = dot(jnp.concatenate(halves(values), axis=1), right)
    return out[:, :width] + out[:, width:]


def lanes_matrix(taps_ref, row, extent, adjoint):
    taps = taps_ref.shape[1]
    source = lax.broadcasted_iota(jnp.int32, (extent, extent), 0)
    target = lax.broadcasted_iota(jnp.int32, (extent, extent), 1)
    offset = (target - source if adjoint else source - target) + taps // 2
    matrix = jnp.zeros((extent, extent), jnp.float32)
    for t in range(taps):
        matrix = jnp.where(offset == t, taps_ref[row, t], matrix)
    high, low = halves(matrix)
    pair = jnp.concatenate([high, low], axis=1)
    return jnp.concatenate([pair, pair], axis=0)


def rows_matrix(taps_ref, row, period, moved, adjoint):
    taps = taps_ref.shape[1]
    target = lax.broadcasted_iota(jnp.int32, (WIDE, WIDE), 0)
    source = lax.broadcasted_iota(jnp.int32, (WIDE, WIDE), 1)
    same = (target // period) == (source // period)
    ahead = target - source if adjoint else source - target
    offset = jnp.bitwise_and(ahead + taps // 2 + moved, period - 1)
    offset = jnp.where(same, offset, taps)
    matrix = jnp.zeros((WIDE, WIDE), jnp.float32)
    for t in range(taps):
        matrix = jnp.where(offset == t, taps_ref[row, t], matrix)
    return halves(matrix)


def pack_kernel(zb, ny, nx, count, perm_ref, image_ref, *refs):
    sends, (turned_ref, tile_ref) = refs[:count], refs[count:]
    reach = 7
    b = lax.axis_index("bulk")
    groups = ny // ROWS

    @pl.when(perm_ref[0] == 1)
    def _():
        edge = jnp.zeros((reach * ROWS, LANES), jnp.float32)
        turned_ref[: reach * ROWS] = edge
        turned_ref[(reach + nx) * ROWS :] = edge
        for tile in range(nx // LANES):
            if nx > LANES:
                tile_ref[...] = image_ref[:, tile * LANES : (tile + 1) * LANES]
                source = tile_ref
            else:
                source = image_ref
            for low in range(ROWS):
                pieces = [
                    source[pl.ds(ROWS * group + low, zb, stride=ny), :]
                    for group in range(groups)
                ]
                block = jnp.concatenate(pieces, axis=0).T
                turned_ref[
                    pl.ds((tile * LANES + reach) * ROWS + low, LANES, stride=ROWS), :
                ] = block
        extent = (zb + 2 * reach) * ROWS
        for d in range(count):
            start = lax.rem(b + d, count) * (zb * ROWS)
            sends[d][:extent] = turned_ref[pl.ds(pl.multiple_of(start, ROWS), extent), :]

    @pl.when(perm_ref[0] != 1)
    def _():
        extent = reach * ny
        for tile in range(nx // LANES):
            lanes = slice(tile * LANES, (tile + 1) * LANES)
            place = slice(tile * extent, (tile + 1) * extent)
            sends[1][place] = image_ref[(zb - reach) * ny :, lanes]
            sends[count - 1][place] = image_ref[:extent, lanes]


def forward_kernel(zb, ny, nx, planes, scalar_ref, taps_ref, estimate_ref, low_ref, high_ref,
                   other_ref, inverse_ref, rows_high_ref, rows_low_ref, lanes_ref, wide_ref):
    taps = taps_ref.shape[1]
    reach = taps // 2
    moved, core = scalar_ref[0], scalar_ref[1]
    wide_ref[pl.ds(reach * core, reach)] = low_ref[...]
    wide_ref[pl.ds(reach * (1 - core), reach)] = other_ref[0]
    wide_ref[2 * reach : 2 * reach + zb] = estimate_ref[...]
    wide_ref[pl.ds(2 * reach + zb + reach * core, reach)] = high_ref[...]
    wide_ref[pl.ds(2 * reach + zb + reach * (1 - core), reach)] = other_ref[1]
    rest = planes - zb - 2 * reach
    wide_ref[4 * reach + zb :] = jnp.zeros((rest, ny, nx), jnp.float32)

    rows_high, rows_low = rows_matrix(taps_ref, 1, ny, moved, False)
    lanes = lanes_matrix(taps_ref, 2, nx, False)
    group = WIDE // ny

    def step(index, carry):
        base = index * group
        blurred = []
        for plane in range(group):
            total = taps_ref[0, 0] * wide_ref[base + plane]
            for t in range(1, taps):
                total = total + taps_ref[0, t] * wide_ref[base + plane + t]
            blurred.append(total)
        values = jnp.concatenate(blurred, axis=0)
        values = blur_lanes(lanes, blur_rows(rows_high, rows_low, values))
        inverse_ref[pl.ds(base, group)] = (1.0 / values).reshape(group, ny, nx)
        return carry

    lax.fori_loop(0, planes // group, step, 0)
    high, low = rows_matrix(taps_ref, 1, ny, moved, True)
    rows_high_ref[...] = high
    rows_low_ref[...] = low
    lanes_ref[...] = lanes_matrix(taps_ref, 2, nx, True)


def adjoint_kernel(zb, ny, nx, count, scalar_ref, taps_ref, visible_ref, image_ref, inverse_ref,
                   rows_high_ref, rows_low_ref, lanes_ref, *refs):
    blocks, (send_ref, keep_ref, ratio_ref, placed_ref) = refs[:count], refs[count:]
    taps = taps_ref.shape[1]
    reach = taps // 2
    core, turned = scalar_ref[1], scalar_ref[2]
    b = lax.axis_index("bulk")
    groups = ny // ROWS
    planes = zb + 2 * reach

    @pl.when(turned == 1)
    def _():
        for d in range(count):
            placed_ref[lax.rem(b + count - d, count)] = blocks[d][: planes * ROWS]
        chunk = 8
        for tile in range(nx // LANES):
            lanes = slice(tile * LANES, (tile + 1) * LANES)
            for first in range(0, planes, chunk):
                size = min(chunk, planes - first)
                spot = lax.broadcasted_iota(jnp.int32, (size * ROWS, LANES), 1) // zb
                parts = [
                    placed_ref[groups * tile + c, first * ROWS : (first + size) * ROWS]
                    for c in range(groups)
                ]
                for g in range(groups):
                    value = None
                    for c in range(groups):
                        shift = (zb * (c - g)) % LANES
                        moved = pltpu.roll(parts[c], shift, 1) if shift else parts[c]
                        value = moved if value is None else jnp.where(spot == c, moved, value)
                    ratio_ref[first : first + size, g * ROWS : (g + 1) * ROWS, lanes] = (
                        value.reshape(size, ROWS, LANES)
                        * inverse_ref[first : first + size, g * ROWS : (g + 1) * ROWS, lanes]
                    )

    @pl.when(turned != 1)
    def _():
        extent = reach * ny
        ratio_ref[reach : reach + zb] = (
            image_ref[...].reshape(zb, ny, nx) * inverse_ref[reach : reach + zb]
        )
        for tile in range(nx // LANES):
            lanes = slice(tile * LANES, (tile + 1) * LANES)
            place = slice(tile * extent, (tile + 1) * extent)
            before = blocks[1][place].reshape(reach, ny, LANES)
            after = blocks[count - 1][place].reshape(reach, ny, LANES)
            before = jnp.where(b > 0, before * inverse_ref[:reach, :, lanes], 0.0)
            after = jnp.where(
                b < count - 1, after * inverse_ref[reach + zb : planes, :, lanes], 0.0
            )
            ratio_ref[:reach, :, lanes] = before
            ratio_ref[reach + zb :, :, lanes] = after

    rows_high, rows_low, lanes_pair = rows_high_ref[...], rows_low_ref[...], lanes_ref[...]
    group = WIDE // ny
    half = zb // 2
    for out_ref, side in ((send_ref, 1 - core), (keep_ref, core)):
        for first in range(0, half, group):
            base = side * half + first
            blurred = []
            for plane in range(group):
                total = taps_ref[0, taps - 1] * ratio_ref[base + plane]
                for t in range(1, taps):
                    total = total + taps_ref[0, taps - 1 - t] * ratio_ref[base + plane + t]
                blurred.append(total)
            values = jnp.concatenate(blurred, axis=0)
            values = blur_lanes(lanes_pair, blur_rows(rows_high, rows_low, values))
            logs = jnp.log(values).reshape(group, ny, nx)
            for plane in range(group):
                weight = jnp.where(visible_ref[base + plane] == 1, 1.0, 0.0)
                out_ref[first + plane] = weight * logs[plane]


def shards(estimate, image, psf, perm, shift, visible):
    zb, ny, nx = estimate.shape
    views, count = lax.axis_size("view"), lax.axis_size("bulk")
    view = lax.axis_index("view")
    core, chip = view % 2, view // 2
    taps = psf.shape[2]
    reach = taps // 2
    kernels = psf[0] / jnp.sum(psf[0], axis=1, keepdims=True)
    joined_taps = jnp.where(perm[0] == 1, kernels[::-1], kernels)
    scalars = jnp.stack([shift[0], core.astype(jnp.int32), perm[0]])
    stack = image[0].reshape(zb * ny, nx)

    extent = max((zb + 2 * reach) * ROWS, reach * ny * (nx // LANES))
    packed = pl.pallas_call(
        functools.partial(pack_kernel, zb, ny, nx, count),
        out_shape=[struct((extent, LANES))] * count,
        in_specs=[SMEM, VMEM],
        out_specs=[VMEM] * count,
        scratch_shapes=[
            pltpu.VMEM(((nx + 2 * reach) * ROWS, LANES), jnp.float32),
            pltpu.VMEM((zb * ny, LANES), jnp.float32),
        ],
        compiler_params=PARAMS,
    )(perm, stack)
    blocks = [packed[0]] + [
        lax.ppermute(packed[d], "bulk", [(i, (i + d) % count) for i in range(count)])
        for d in range(1, count)
    ]

    swap = [(i, i ^ 1) for i in range(views)]
    forward = [(i, i + 1) for i in range(count - 1)]
    backward = [(i + 1, i) for i in range(count - 1)]
    low = lax.ppermute(
        lax.dynamic_slice_in_dim(estimate, zb - 2 * reach + reach * core, reach, 0),
        "bulk", forward,
    )
    high = lax.ppermute(
        lax.dynamic_slice_in_dim(estimate, reach * core, reach, 0), "bulk", backward
    )
    other = lax.ppermute(jnp.stack([low, high]), "view", swap)

    group = WIDE // ny
    planes = -(-(zb + 2 * reach) // group) * group
    inverse, rows_high, rows_low, lanes_pair = pl.pallas_call(
        functools.partial(forward_kernel, zb, ny, nx, planes),
        out_shape=[
            struct((planes, ny, nx)),
            struct((WIDE, WIDE), jnp.bfloat16),
            struct((WIDE, WIDE), jnp.bfloat16),
            struct((2 * nx, 2 * nx), jnp.bfloat16),
        ],
        in_specs=[SMEM, SMEM] + [VMEM] * 4,
        out_specs=[VMEM] * 4,
        scratch_shapes=[pltpu.VMEM((planes + 2 * reach, ny, nx), jnp.float32)],
        compiler_params=PARAMS,
    )(scalars, joined_taps, estimate, low, high, other)

    half = zb // 2
    send, keep = pl.pallas_call(
        functools.partial(adjoint_kernel, zb, ny, nx, count),
        out_shape=[struct((half, ny, nx))] * 2,
        in_specs=[SMEM] * 3 + [VMEM] * (5 + count),
        out_specs=[VMEM] * 2,
        scratch_shapes=[
            pltpu.VMEM((zb + 2 * reach, ny, nx), jnp.float32),
            pltpu.VMEM((count, (zb + 2 * reach) * ROWS, LANES), jnp.float32),
        ],
        compiler_params=PARAMS,
    )(scalars, joined_taps, visible[0], stack, inverse, rows_high, rows_low, lanes_pair, *blocks)

    chips = views // 2
    piece = half // chips
    summed = keep + lax.ppermute(send, "view", swap)
    total = lax.dynamic_slice_in_dim(summed, chip * piece, piece, 0)
    partners = [[(i, i ^ (2 * d)) for i in range(views)] for d in range(1, chips)]
    arrived = [
        lax.ppermute(
            lax.dynamic_slice_in_dim(summed, (chip ^ (d + 1)) * piece, piece, 0), "view", pairs
        )
        for d, pairs in enumerate(partners)
    ]
    for part in arrived:
        total = total + part
    mine = lax.dynamic_slice_in_dim(estimate, core * half + chip * piece, piece, 0)
    mine = mine * jnp.exp(total / float(views))
    own = jnp.zeros((half, ny, nx), jnp.float32)
    own = lax.dynamic_update_slice_in_dim(own, mine, chip * piece, 0)
    for d, pairs in enumerate(partners):
        part = lax.ppermute(mine, "view", pairs)
        own = lax.dynamic_update_slice_in_dim(own, part, (chip ^ (d + 1)) * piece, 0)
    their = lax.ppermute(own, "view", swap)
    return jnp.concatenate(
        [jnp.where(core == 0, own, their), jnp.where(core == 0, their, own)], axis=0
    )


def solution(mesh):
    placed = (
        P("bulk", None, None),
        P("view", "bulk", None, None),
        P("view", None, None),
        P("view"),
        P("view"),
        P("view", "bulk"),
    )
    return jax.shard_map(
        shards, mesh=mesh, in_specs=placed, out_specs=P("bulk", None, None), check_vma=False
    )
```

```python
import functools

import jax
import jax.numpy as jnp
from jax import lax
from jax.experimental import pallas as pl
from jax.experimental.pallas import tpu as pltpu
from jax.sharding import PartitionSpec as P

LANES = 128
ROWS = 8
WIDE = 256
VMEM = pl.BlockSpec(memory_space=pltpu.VMEM)
SMEM = pl.BlockSpec(memory_space=pltpu.SMEM)
PARAMS = pltpu.CompilerParams(vmem_limit_bytes=40 * 1024 * 1024)


def struct(shape, dtype=jnp.float32):
    return jax.ShapeDtypeStruct(shape, dtype)


def halves(values):
    high = values.astype(jnp.bfloat16)
    low = (values - high.astype(jnp.float32)).astype(jnp.bfloat16)
    return high, low


def dot(left, right):
    return jnp.dot(left, right, preferred_element_type=jnp.float32)


def blur_rows(left_high, left_low, values):
    width = values.shape[1]
    high, low = halves(values)
    both = dot(left_high, jnp.concatenate([high, low], axis=1))
    return both[:, :width] + both[:, width:] + dot(left_low, high)


def blur_lanes(right, values):
    width = values.shape[1]
    out = dot(jnp.concatenate(halves(values), axis=1), right)
    return out[:, :width] + out[:, width:]


def lanes_matrix(taps_ref, row, extent, adjoint):
    taps = taps_ref.shape[1]
    source = lax.broadcasted_iota(jnp.int32, (extent, extent), 0)
    target = lax.broadcasted_iota(jnp.int32, (extent, extent), 1)
    offset = (target - source if adjoint else source - target) + taps // 2
    matrix = jnp.zeros((extent, extent), jnp.float32)
    for t in range(taps):
        matrix = jnp.where(offset == t, taps_ref[row, t], matrix)
    high, low = halves(matrix)
    pair = jnp.concatenate([high, low], axis=1)
    return jnp.concatenate([pair, pair], axis=0)


def rows_matrix(taps_ref, row, period, moved, adjoint):
    taps = taps_ref.shape[1]
    target = lax.broadcasted_iota(jnp.int32, (WIDE, WIDE), 0)
    source = lax.broadcasted_iota(jnp.int32, (WIDE, WIDE), 1)
    same = (target // period) == (source // period)
    ahead = target - source if adjoint else source - target
    offset = jnp.bitwise_and(ahead + taps // 2 + moved, period - 1)
    offset = jnp.where(same, offset, taps)
    matrix = jnp.zeros((WIDE, WIDE), jnp.float32)
    for t in range(taps):
        matrix = jnp.where(offset == t, taps_ref[row, t], matrix)
    return halves(matrix)


def pack_kernel(zb, ny, nx, count, perm_ref, image_ref, *refs):
    sends, (turned_ref, tile_ref) = refs[:count], refs[count:]
    reach = 7
    b = lax.axis_index("bulk")
    groups = ny // ROWS

    @pl.when(perm_ref[0] == 1)
    def _():
        edge = jnp.zeros((reach * ROWS, LANES), jnp.float32)
        turned_ref[: reach * ROWS] = edge
        turned_ref[(reach + nx) * ROWS :] = edge
        for tile in range(nx // LANES):
            if nx > LANES:
                tile_ref[...] = image_ref[:, tile * LANES : (tile + 1) * LANES]
                source = tile_ref
            else:
                source = image_ref
            for low in range(ROWS):
                pieces = [
                    source[pl.ds(ROWS * group + low, zb, stride=ny), :]
                    for group in range(groups)
                ]
                block = jnp.concatenate(pieces, axis=0).T
                turned_ref[
                    pl.ds((tile * LANES + reach) * ROWS + low, LANES, stride=ROWS), :
                ] = block
        extent = (zb + 2 * reach) * ROWS
        for d in range(count):
            start = lax.rem(b + d, count) * (zb * ROWS)
            sends[d][:extent] = turned_ref[pl.ds(pl.multiple_of(start, ROWS), extent), :]

    @pl.when(perm_ref[0] != 1)
    def _():
        extent = reach * ny
        for tile in range(nx // LANES):
            lanes = slice(tile * LANES, (tile + 1) * LANES)
            place = slice(tile * extent, (tile + 1) * extent)
            sends[1][place] = image_ref[(zb - reach) * ny :, lanes]
            sends[count - 1][place] = image_ref[:extent, lanes]


def forward_kernel(zb, ny, nx, planes, scalar_ref, taps_ref, estimate_ref, low_ref, high_ref,
                   other_ref, inverse_ref, rows_high_ref, rows_low_ref, lanes_ref, wide_ref):
    taps = taps_ref.shape[1]
    reach = taps // 2
    moved, core = scalar_ref[0], scalar_ref[1]
    wide_ref[pl.ds(reach * core, reach)] = low_ref[...]
    wide_ref[pl.ds(reach * (1 - core), reach)] = other_ref[0]
    wide_ref[2 * reach : 2 * reach + zb] = estimate_ref[...]
    wide_ref[pl.ds(2 * reach + zb + reach * core, reach)] = high_ref[...]
    wide_ref[pl.ds(2 * reach + zb + reach * (1 - core), reach)] = other_ref[1]
    rest = planes - zb - 2 * reach
    wide_ref[4 * reach + zb :] = jnp.zeros((rest, ny, nx), jnp.float32)

    rows_high, rows_low = rows_matrix(taps_ref, 1, ny, moved, False)
    lanes = lanes_matrix(taps_ref, 2, nx, False)
    group = WIDE // ny

    def step(index, carry):
        base = index * group
        blurred = []
        for plane in range(group):
            total = taps_ref[0, 0] * wide_ref[base + plane]
            for t in range(1, taps):
                total = total + taps_ref[0, t] * wide_ref[base + plane + t]
            blurred.append(total)
        values = jnp.concatenate(blurred, axis=0)
        values = blur_lanes(lanes, blur_rows(rows_high, rows_low, values))
        inverse_ref[pl.ds(base, group)] = (1.0 / values).reshape(group, ny, nx)
        return carry

    lax.fori_loop(0, planes // group, step, 0)
    high, low = rows_matrix(taps_ref, 1, ny, moved, True)
    rows_high_ref[...] = high
    rows_low_ref[...] = low
    lanes_ref[...] = lanes_matrix(taps_ref, 2, nx, True)


def adjoint_kernel(zb, ny, nx, count, scalar_ref, taps_ref, visible_ref, image_ref, inverse_ref,
                   rows_high_ref, rows_low_ref, lanes_ref, *refs):
    blocks, (send_ref, keep_ref, ratio_ref, placed_ref) = refs[:count], refs[count:]
    taps = taps_ref.shape[1]
    reach = taps // 2
    core, turned = scalar_ref[1], scalar_ref[2]
    b = lax.axis_index("bulk")
    groups = ny // ROWS
    planes = zb + 2 * reach

    @pl.when(turned == 1)
    def _():
        for d in range(count):
            placed_ref[lax.rem(b + count - d, count)] = blocks[d][: planes * ROWS]
        chunk = 8
        for tile in range(nx // LANES):
            lanes = slice(tile * LANES, (tile + 1) * LANES)
            for first in range(0, planes, chunk):
                size = min(chunk, planes - first)
                spot = lax.broadcasted_iota(jnp.int32, (size * ROWS, LANES), 1) // zb
                parts = [
                    placed_ref[groups * tile + c, first * ROWS : (first + size) * ROWS]
                    for c in range(groups)
                ]
                for g in range(groups):
                    value = None
                    for c in range(groups):
                        shift = (zb * (c - g)) % LANES
                        moved = pltpu.roll(parts[c], shift, 1) if shift else parts[c]
                        value = moved if value is None else jnp.where(spot == c, moved, value)
                    ratio_ref[first : first + size, g * ROWS : (g + 1) * ROWS, lanes] = (
                        value.reshape(size, ROWS, LANES)
                        * inverse_ref[first : first + size, g * ROWS : (g + 1) * ROWS, lanes]
                    )

    @pl.when(turned != 1)
    def _():
        extent = reach * ny
        ratio_ref[reach : reach + zb] = (
            image_ref[...].reshape(zb, ny, nx) * inverse_ref[reach : reach + zb]
        )
        for tile in range(nx // LANES):
            lanes = slice(tile * LANES, (tile + 1) * LANES)
            place = slice(tile * extent, (tile + 1) * extent)
            before = blocks[1][place].reshape(reach, ny, LANES)
            after = blocks[count - 1][place].reshape(reach, ny, LANES)
            before = jnp.where(b > 0, before * inverse_ref[:reach, :, lanes], 0.0)
            after = jnp.where(
                b < count - 1, after * inverse_ref[reach + zb : planes, :, lanes], 0.0
            )
            ratio_ref[:reach, :, lanes] = before
            ratio_ref[reach + zb :, :, lanes] = after

    rows_high, rows_low, lanes_pair = rows_high_ref[...], rows_low_ref[...], lanes_ref[...]
    group = WIDE // ny
    half = zb // 2
    for out_ref, side in ((send_ref, 1 - core), (keep_ref, core)):
        for first in range(0, half, group):
            base = side * half + first
            blurred = []
            for plane in range(group):
                total = taps_ref[0, taps - 1] * ratio_ref[base + plane]
                for t in range(1, taps):
                    total = total + taps_ref[0, taps - 1 - t] * ratio_ref[base + plane + t]
                blurred.append(total)
            values = jnp.concatenate(blurred, axis=0)
            values = blur_lanes(lanes_pair, blur_rows(rows_high, rows_low, values))
            logs = jnp.log(values).reshape(group, ny, nx)
            for plane in range(group):
                weight = jnp.where(visible_ref[base + plane] == 1, 1.0, 0.0)
                out_ref[first + plane] = weight * logs[plane]


def shards(estimate, image, psf, perm, shift, visible):
    zb, ny, nx = estimate.shape
    views, count = lax.axis_size("view"), lax.axis_size("bulk")
    view = lax.axis_index("view")
    core, chip = view % 2, view // 2
    taps = psf.shape[2]
    reach = taps // 2
    kernels = psf[0] / jnp.sum(psf[0], axis=1, keepdims=True)
    joined_taps = jnp.where(perm[0] == 1, kernels[::-1], kernels)
    scalars = jnp.stack([shift[0], core.astype(jnp.int32), perm[0]])
    stack = image[0].reshape(zb * ny, nx)

    extent = max((zb + 2 * reach) * ROWS, reach * ny * (nx // LANES))
    packed = pl.pallas_call(
        functools.partial(pack_kernel, zb, ny, nx, count),
        out_shape=[struct((extent, LANES))] * count,
        in_specs=[SMEM, VMEM],
        out_specs=[VMEM] * count,
        scratch_shapes=[
            pltpu.VMEM(((nx + 2 * reach) * ROWS, LANES), jnp.float32),
            pltpu.VMEM((zb * ny, LANES), jnp.float32),
        ],
        compiler_params=PARAMS,
    )(perm, stack)
    blocks = [packed[0]] + [
        lax.ppermute(packed[d], "bulk", [(i, (i + d) % count) for i in range(count)])
        for d in range(1, count)
    ]

    swap = [(i, i ^ 1) for i in range(views)]
    forward = [(i, i + 1) for i in range(count - 1)]
    backward = [(i + 1, i) for i in range(count - 1)]
    later, _ = lax.optimization_barrier((estimate, packed[1]))
    low = lax.ppermute(
        lax.dynamic_slice_in_dim(later, zb - 2 * reach + reach * core, reach, 0),
        "bulk", forward,
    )
    high = lax.ppermute(
        lax.dynamic_slice_in_dim(later, reach * core, reach, 0), "bulk", backward
    )
    other = lax.ppermute(jnp.stack([low, high]), "view", swap)

    group = WIDE // ny
    planes = -(-(zb + 2 * reach) // group) * group
    inverse, rows_high, rows_low, lanes_pair = pl.pallas_call(
        functools.partial(forward_kernel, zb, ny, nx, planes),
        out_shape=[
            struct((planes, ny, nx)),
            struct((WIDE, WIDE), jnp.bfloat16),
            struct((WIDE, WIDE), jnp.bfloat16),
            struct((2 * nx, 2 * nx), jnp.bfloat16),
        ],
        in_specs=[SMEM, SMEM] + [VMEM] * 4,
        out_specs=[VMEM] * 4,
        scratch_shapes=[pltpu.VMEM((planes + 2 * reach, ny, nx), jnp.float32)],
        compiler_params=PARAMS,
    )(scalars, joined_taps, estimate, low, high, other)

    half = zb // 2
    send, keep = pl.pallas_call(
        functools.partial(adjoint_kernel, zb, ny, nx, count),
        out_shape=[struct((half, ny, nx))] * 2,
        in_specs=[SMEM] * 3 + [VMEM] * (5 + count),
        out_specs=[VMEM] * 2,
        scratch_shapes=[
            pltpu.VMEM((zb + 2 * reach, ny, nx), jnp.float32),
            pltpu.VMEM((count, (zb + 2 * reach) * ROWS, LANES), jnp.float32),
        ],
        compiler_params=PARAMS,
    )(scalars, joined_taps, visible[0], stack, inverse, rows_high, rows_low, lanes_pair, *blocks)

    total = keep + lax.ppermute(send, "view", swap)
    bits = (views // 2).bit_length() - 1
    for step in range(bits):
        flips = [2 << step, 2 << ((step + bits - 1) % bits)]
        total = total + lax.ppermute(
            total, "view", [(i, i ^ flips[i % 2]) for i in range(views)]
        )
    own = lax.dynamic_slice_in_dim(estimate, core * half, half, 0)
    own = own * jnp.exp(total / float(views))
    their = lax.ppermute(own, "view", swap)
    return jnp.concatenate(
        [jnp.where(core == 0, own, their), jnp.where(core == 0, their, own)], axis=0
    )


def solution(mesh):
    placed = (
        P("bulk", None, None),
        P("view", "bulk", None, None),
        P("view", None, None),
        P("view"),
        P("view"),
        P("view", "bulk"),
    )
    return jax.shard_map(
        shards, mesh=mesh, in_specs=placed, out_specs=P("bulk", None, None), check_vma=False
    )
```

```python
import functools

import jax
import jax.numpy as jnp
from jax import lax
from jax.experimental import pallas as pl
from jax.experimental.pallas import tpu as pltpu
from jax.sharding import PartitionSpec as P

LANES = 128
ROWS = 8
WIDE = 256
VMEM = pl.BlockSpec(memory_space=pltpu.VMEM)
SMEM = pl.BlockSpec(memory_space=pltpu.SMEM)
COST = pl.CostEstimate(flops=2**29, bytes_accessed=2**21, transcendentals=2**16)
PARAMS = pltpu.CompilerParams(vmem_limit_bytes=40 * 1024 * 1024)


def struct(shape, dtype=jnp.float32):
    return jax.ShapeDtypeStruct(shape, dtype)


def halves(values):
    high = values.astype(jnp.bfloat16)
    low = (values - high.astype(jnp.float32)).astype(jnp.bfloat16)
    return high, low


def dot(left, right):
    return jnp.dot(left, right, preferred_element_type=jnp.float32)


def blur_rows(left_high, left_low, values):
    width = values.shape[1]
    high, low = halves(values)
    both = dot(left_high, jnp.concatenate([high, low], axis=1))
    return both[:, :width] + both[:, width:] + dot(left_low, high)


def blur_lanes(right, values):
    width = values.shape[1]
    out = dot(jnp.concatenate(halves(values), axis=1), right)
    return out[:, :width] + out[:, width:]


def lanes_matrix(taps_ref, row, extent, adjoint):
    taps = taps_ref.shape[1]
    source = lax.broadcasted_iota(jnp.int32, (extent, extent), 0)
    target = lax.broadcasted_iota(jnp.int32, (extent, extent), 1)
    offset = (target - source if adjoint else source - target) + taps // 2
    matrix = jnp.zeros((extent, extent), jnp.float32)
    for t in range(taps):
        matrix = jnp.where(offset == t, taps_ref[row, t], matrix)
    high, low = halves(matrix)
    pair = jnp.concatenate([high, low], axis=1)
    return jnp.concatenate([pair, pair], axis=0)


def rows_matrix(taps_ref, row, period, moved, adjoint):
    taps = taps_ref.shape[1]
    target = lax.broadcasted_iota(jnp.int32, (period, WIDE), 0)
    source = lax.broadcasted_iota(jnp.int32, (period, WIDE), 1)
    ahead = target - source if adjoint else source - target
    offset = jnp.bitwise_and(ahead + taps // 2 + moved, period - 1)
    block = jnp.zeros((period, WIDE), jnp.float32)
    for t in range(taps):
        block = jnp.where(offset == t, taps_ref[row, t], block)
    plane = source // period
    return halves(
        jnp.concatenate([jnp.where(plane == p, block, 0.0) for p in range(WIDE // period)], axis=0)
    )


def blur_planes(source_ref, splats, base, group):
    ny, nx = source_ref.shape[1:]
    taps = len(splats)
    columns = []
    for tile in range(nx // LANES):
        lanes = slice(tile * LANES, (tile + 1) * LANES)
        places = []
        for row in range(ny // ROWS):
            rows = slice(row * ROWS, (row + 1) * ROWS)
            source = [source_ref[base + i, rows, lanes] for i in range(group + taps - 1)]
            sums = []
            for plane in range(group):
                total = splats[0] * source[plane]
                for t in range(1, taps):
                    total = total + splats[t] * source[plane + t]
                sums.append(total)
            places.append(sums)
        columns.append(
            jnp.concatenate([sums[plane] for plane in range(group) for sums in places], axis=0)
        )
    return columns[0] if len(columns) == 1 else jnp.concatenate(columns, axis=1)


def pack_kernel(zb, ny, nx, count, image_ref, *refs):
    sends, (turned_ref, tile_ref) = refs[:count], refs[count:]
    reach = 7
    b = lax.axis_index("bulk")
    groups = ny // ROWS
    extent = (zb + 2 * reach) * ROWS
    edge = jnp.zeros((reach * ROWS, LANES), jnp.float32)
    turned_ref[: reach * ROWS] = edge
    turned_ref[(reach + nx) * ROWS :] = edge
    for tile in range(nx // LANES):
        if nx > LANES:
            tile_ref[...] = image_ref[:, tile * LANES : (tile + 1) * LANES]
            source = tile_ref
        else:
            source = image_ref
        for low in range(ROWS):
            pieces = [
                source[pl.ds(ROWS * group + low, zb, stride=ny), :] for group in range(groups)
            ]
            block = jnp.concatenate(pieces, axis=0).T
            turned_ref[pl.ds((tile * LANES + reach) * ROWS + low, LANES, stride=ROWS), :] = block
    for k in range(count):
        start = jnp.bitwise_xor(b, k) * (zb * ROWS)
        sends[k][...] = turned_ref[pl.ds(pl.multiple_of(start, ROWS), extent), :]


def forward_kernel(zb, ny, nx, planes, scalar_ref, taps_ref, visible_ref, estimate_ref, near1_ref,
                   near2_ref, other_ref, inverse_ref, rows_high_ref, rows_low_ref, lanes_ref,
                   weight_ref, splat_ref, flag_ref,
                   wide_ref):
    taps = taps_ref.shape[1]
    reach = taps // 2
    moved, core = scalar_ref[0], scalar_ref[1]
    flag_ref[...] = jnp.full((ROWS, LANES), scalar_ref[2], jnp.int32)
    wide_ref[2 * reach : 2 * reach + zb] = estimate_ref[...]
    odd = lax.rem(lax.axis_index("bulk"), 2)
    for side, (near_ref, far_side) in enumerate(((near1_ref, 1 - odd), (near2_ref, odd))):
        first = far_side * (2 * reach + zb)
        wide_ref[pl.ds(first + reach * core, reach)] = near_ref[...]
        wide_ref[pl.ds(first + reach * (1 - core), reach)] = other_ref[side]
    rest = planes - zb - 2 * reach
    wide_ref[4 * reach + zb :] = jnp.zeros((rest, ny, nx), jnp.float32)

    rows_high, rows_low = rows_matrix(taps_ref, 1, ny, moved, False)
    lanes = lanes_matrix(taps_ref, 2, nx, False)
    group = WIDE // ny

    tile = (ROWS, LANES)
    splats = [jnp.full(tile, taps_ref[0, t], jnp.float32) for t in range(taps)]
    for t in range(taps):
        splat_ref[taps - 1 - t] = splats[t]
    for base in range(0, planes, group):
        values = blur_planes(wide_ref, splats, base, group)
        values = blur_lanes(lanes, blur_rows(rows_high, rows_low, values))
        inverse_ref[base : base + group] = (1.0 / values).reshape(group, ny, nx)
    high, low = rows_matrix(taps_ref, 1, ny, moved, True)
    rows_high_ref[...] = high
    rows_low_ref[...] = low
    lanes_ref[...] = lanes_matrix(taps_ref, 2, nx, True)
    for plane in range(zb):
        weight = jnp.where(visible_ref[plane] == 1, 1.0, 0.0)
        weight_ref[plane] = jnp.full((ROWS, LANES), weight, jnp.float32)


def neighbours(count):
    return [k for k in range(1, count) if k & (k + 1) == 0]


def beside_in(b, k):
    low = jnp.bitwise_and(b, k)
    return jnp.logical_or(low == k // 2, low == k // 2 + 1)


def ratio_kernel(zb, ny, nx, count, flag_ref, weight_ref, splat_ref, image_ref, inverse_ref,
                 rows_high_ref, rows_low_ref, lanes_ref, *refs):
    blocks, (send_ref, keep_ref, ratio_ref, placed_ref) = refs[:count], refs[count:]
    reach = splat_ref.shape[0] // 2
    b = lax.axis_index("bulk")
    groups = ny // ROWS
    planes = zb + 2 * reach
    turned = flag_ref[...] == 1
    for k in range(count):
        placed_ref[jnp.bitwise_xor(b, k)] = blocks[k][: planes * ROWS]
    odd = lax.rem(b, 2) == 1
    spot = lax.broadcasted_iota(jnp.int32, (ROWS, LANES), 1) // zb
    outside = {0: b > 0, reach + zb: b < count - 1}
    for tile in range(nx // LANES):
        lanes = slice(tile * LANES, (tile + 1) * LANES)
        for plane in range(planes):
            place = slice(plane * ROWS, (plane + 1) * ROWS)
            pieces = [placed_ref[groups * tile + c, place] for c in range(groups)]
            for g in range(groups):
                rows = slice(g * ROWS, (g + 1) * ROWS)
                value = None
                for c in range(groups):
                    shift = (zb * (c - g)) % LANES
                    moved = pltpu.roll(pieces[c], shift, 1) if shift else pieces[c]
                    value = moved if value is None else jnp.where(spot == c, moved, value)
                if reach <= plane < reach + zb:
                    start = (plane - reach) * ny + g * ROWS
                    straight = image_ref[start : start + ROWS, lanes]
                else:
                    side = 0 if plane < reach else reach + zb
                    start = (tile * reach + plane - side) * ny + g * ROWS
                    beside = [blocks[k][start : start + ROWS] for k in neighbours(count)]
                    far = beside[1]
                    for k, value2 in zip(neighbours(count)[2:], beside[2:]):
                        far = jnp.where(beside_in(b, k), value2, far)
                    straight = jnp.where(odd == (side == 0), beside[0], far)
                    straight = jnp.where(outside[side], straight, 0.0)
                value = jnp.where(turned, value, straight)
                ratio_ref[plane, rows, lanes] = value * inverse_ref[plane, rows, lanes]

    adjoint_kernel(0, weight_ref, splat_ref, ratio_ref, rows_high_ref, rows_low_ref, lanes_ref,
                   send_ref, keep_ref)


def adjoint_kernel(part, weight_ref, splat_ref, ratio_ref, rows_high_ref, rows_low_ref, lanes_ref,
                   send_ref, keep_ref):
    core = lax.rem(lax.axis_index("view"), 2)
    splats = [splat_ref[t] for t in range(splat_ref.shape[0])]
    rows_high, rows_low, lanes_pair = rows_high_ref[...], rows_low_ref[...], lanes_ref[...]
    size, ny, nx = send_ref.shape
    group = WIDE // ny
    for out_ref, side in ((send_ref, 1 - core), (keep_ref, core)):
        for first in range(0, size, group):
            base = (2 * part + side) * size + first
            values = blur_planes(ratio_ref, splats, base, group)
            values = blur_lanes(lanes_pair, blur_rows(rows_high, rows_low, values))
            logs = jnp.log(values).reshape(group, ny // ROWS, ROWS, nx)
            for plane in range(group):
                weight = weight_ref[base + plane]
                for tile in range(nx // LANES):
                    lanes = slice(tile * LANES, (tile + 1) * LANES)
                    for row in range(ny // ROWS):
                        out_ref[first + plane, row * ROWS : (row + 1) * ROWS, lanes] = (
                            weight * logs[plane, row, :, lanes]
                        )


def shards(estimate, image, psf, perm, shift, visible):
    zb, ny, nx = estimate.shape
    views, count = lax.axis_size("view"), lax.axis_size("bulk")
    view = lax.axis_index("view")
    core, chip = view % 2, view // 2
    taps = psf.shape[2]
    reach = taps // 2
    kernels = psf[0] / jnp.sum(psf[0], axis=1, keepdims=True)
    stack = image[0].reshape(zb * ny, nx)

    tiles = nx // LANES
    halo = reach * ny
    extent = (zb + 2 * reach) * ROWS
    packed = list(pl.pallas_call(
        functools.partial(pack_kernel, zb, ny, nx, count),
        out_shape=[struct((extent, LANES))] * count,
        in_specs=[VMEM],
        out_specs=[VMEM] * count,
        scratch_shapes=[
            pltpu.VMEM(((nx + 2 * reach) * ROWS, LANES), jnp.float32),
            pltpu.VMEM((zb * ny, LANES), jnp.float32),
        ],
        compiler_params=PARAMS,
    )(stack))
    late_perm, _ = lax.optimization_barrier((perm, packed[1]))
    length = max(extent, halo * tiles)

    bulk = lax.axis_index("bulk")
    even = bulk % 2 == 0

    def beside(first):
        planes = lax.dynamic_slice_in_dim(stack, first, halo, 0).reshape(halo, tiles, LANES)
        planes = jnp.swapaxes(planes, 0, 1).reshape(halo * tiles, LANES)
        return jnp.pad(planes, ((0, length - halo * tiles), (0, 0)))

    for k in neighbours(count):
        block = jnp.pad(packed[k], ((0, length - extent), (0, 0)))
        above = even if k == 1 else jnp.logical_not(even)
        start = jnp.where(above, (zb - reach) * ny, 0)
        packed[k] = jnp.where(late_perm[0] == 1, block, beside(start))
    blocks = {0: packed[0]}
    for k in range(count - 1, 0, -1):
        blocks[k] = lax.ppermute(packed[k], "bulk", [(i, i ^ k) for i in range(count)])
    blocks = [blocks[k] for k in range(count)]

    joined_taps = jnp.where(late_perm[0] == 1, kernels[::-1], kernels)
    scalars = jnp.stack([shift[0], core.astype(jnp.int32), late_perm[0]])

    swap = [(i, i ^ 1) for i in range(views)]
    later, *_ = lax.optimization_barrier((estimate, packed[count - 1]))
    near = []
    for k in neighbours(count):
        above = even if k == 1 else jnp.logical_not(even)
        start = jnp.where(above, zb - 2 * reach, 0) + reach * core
        pairs = [(i, i ^ k) for i in range(count) if abs(i - (i ^ k)) == 1]
        near.append(
            lax.ppermute(lax.dynamic_slice_in_dim(later, start, reach, 0), "bulk", pairs)
        )
    near = [near[0], sum(near[2:], near[1])]
    other = lax.ppermute(jnp.stack(near), "view", swap)

    group = WIDE // ny
    planes = -(-(zb + 2 * reach) // group) * group
    inverse, rows_high, rows_low, lanes_pair, weight, splats, flags = pl.pallas_call(
        functools.partial(forward_kernel, zb, ny, nx, planes),
        out_shape=[
            struct((planes, ny, nx)),
            struct((WIDE, WIDE), jnp.bfloat16),
            struct((WIDE, WIDE), jnp.bfloat16),
            struct((2 * nx, 2 * nx), jnp.bfloat16),
            struct((zb, ROWS, LANES)),
            struct((taps, ROWS, LANES)),
            struct((ROWS, LANES), jnp.int32),
        ],
        in_specs=[SMEM] * 3 + [VMEM] * 4,
        out_specs=[VMEM] * 7,
        scratch_shapes=[pltpu.VMEM((planes + 2 * reach, ny, nx), jnp.float32)],
        compiler_params=PARAMS,
    )(scalars, joined_taps, visible[0], estimate, *near, other)

    parts = 2
    size = zb // (2 * parts)
    matrices = (rows_high, rows_low, lanes_pair)
    first = pl.pallas_call(
        functools.partial(ratio_kernel, zb, ny, nx, count),
        out_shape=[struct((size, ny, nx))] * 2 + [struct((zb + 2 * reach, ny, nx))],
        in_specs=[VMEM] * (8 + count),
        out_specs=[VMEM] * 3,
        scratch_shapes=[
            pltpu.VMEM((count, (zb + 2 * reach) * ROWS, LANES), jnp.float32),
        ],
        compiler_params=PARAMS,
    )(flags, weight, splats, stack, inverse, *matrices, *blocks)
    total = [first[1] + lax.ppermute(first[0], "view", swap)]
    for part in range(1, parts):
        held, total[-1] = lax.optimization_barrier((weight, total[-1]))
        send, keep = pl.pallas_call(
            functools.partial(adjoint_kernel, part),
            out_shape=[struct((size, ny, nx))] * 2,
            in_specs=[VMEM] * 6,
            out_specs=[VMEM] * 2,
            cost_estimate=COST,
            compiler_params=PARAMS,
        )(held, splats, first[2], *matrices)
        total.append(keep + lax.ppermute(send, "view", swap))

    bits = (views // 2).bit_length() - 1
    result = []
    for part in range(parts):
        for step in range(bits):
            flips = [2 << step, 2 << ((step + bits - 1) % bits)]
            total[part] = total[part] + lax.ppermute(
                total[part], "view", [(i, i ^ flips[i % 2]) for i in range(views)]
            )
        own = lax.dynamic_slice_in_dim(estimate, (2 * part + core) * size, size, 0)
        own = own * jnp.exp(total[part] / float(views))
        their = lax.ppermute(own, "view", swap)
        result += [jnp.where(core == 0, own, their), jnp.where(core == 0, their, own)]
    return jnp.concatenate(result, axis=0)


def solution(mesh):
    placed = (
        P("bulk", None, None),
        P("view", "bulk", None, None),
        P("view", None, None),
        P("view"),
        P("view"),
        P("view", "bulk"),
    )
    return jax.shard_map(
        shards, mesh=mesh, in_specs=placed, out_specs=P("bulk", None, None), check_vma=False
    )
```

```python
import functools

import jax
import jax.numpy as jnp
from jax import lax
from jax.experimental import pallas as pl
from jax.experimental.pallas import tpu as pltpu
from jax.sharding import PartitionSpec as P

LANES = 128
ROWS = 8
WIDE = 256
VMEM = pl.BlockSpec(memory_space=pltpu.VMEM)
SMEM = pl.BlockSpec(memory_space=pltpu.SMEM)
COST = pl.CostEstimate(flops=2**29, bytes_accessed=2**21, transcendentals=2**16)
PARAMS = pltpu.CompilerParams(vmem_limit_bytes=40 * 1024 * 1024)


def struct(shape, dtype=jnp.float32):
    return jax.ShapeDtypeStruct(shape, dtype)


def halves(values):
    high = values.astype(jnp.bfloat16)
    low = (values - high.astype(jnp.float32)).astype(jnp.bfloat16)
    return high, low


def dot(left, right):
    return jnp.dot(left, right, preferred_element_type=jnp.float32)


def blur_rows(left_high, left_low, values):
    width = values.shape[1]
    high, low = halves(values)
    both = dot(left_high, jnp.concatenate([high, low], axis=1))
    return both[:, :width] + both[:, width:] + dot(left_low, high)


def blur_lanes(right, values):
    width = values.shape[1]
    out = dot(jnp.concatenate(halves(values), axis=1), right)
    return out[:, :width] + out[:, width:]


def lanes_matrix(taps_ref, row, extent, adjoint):
    taps = taps_ref.shape[1]
    source = lax.broadcasted_iota(jnp.int32, (extent, extent), 0)
    target = lax.broadcasted_iota(jnp.int32, (extent, extent), 1)
    offset = (target - source if adjoint else source - target) + taps // 2
    matrix = jnp.zeros((extent, extent), jnp.float32)
    for t in range(taps):
        matrix = jnp.where(offset == t, taps_ref[row, t], matrix)
    high, low = halves(matrix)
    pair = jnp.concatenate([high, low], axis=1)
    return jnp.concatenate([pair, pair], axis=0)


def rows_matrix(taps_ref, row, period, moved, adjoint):
    taps = taps_ref.shape[1]
    target = lax.broadcasted_iota(jnp.int32, (period, WIDE), 0)
    source = lax.broadcasted_iota(jnp.int32, (period, WIDE), 1)
    ahead = target - source if adjoint else source - target
    offset = jnp.bitwise_and(ahead + taps // 2 + moved, period - 1)
    block = jnp.zeros((period, WIDE), jnp.float32)
    for t in range(taps):
        block = jnp.where(offset == t, taps_ref[row, t], block)
    plane = source // period
    return halves(
        jnp.concatenate([jnp.where(plane == p, block, 0.0) for p in range(WIDE // period)], axis=0)
    )


def blur_planes(source_ref, splats, base, group):
    ny, nx = source_ref.shape[1:]
    taps = len(splats)
    columns = []
    for tile in range(nx // LANES):
        lanes = slice(tile * LANES, (tile + 1) * LANES)
        places = []
        for row in range(ny // ROWS):
            rows = slice(row * ROWS, (row + 1) * ROWS)
            source = [source_ref[base + i, rows, lanes] for i in range(group + taps - 1)]
            sums = []
            for plane in range(group):
                total = splats[0] * source[plane]
                for t in range(1, taps):
                    total = total + splats[t] * source[plane + t]
                sums.append(total)
            places.append(sums)
        columns.append(
            jnp.concatenate([sums[plane] for plane in range(group) for sums in places], axis=0)
        )
    return columns[0] if len(columns) == 1 else jnp.concatenate(columns, axis=1)


def pack_kernel(zb, ny, nx, count, image_ref, *refs):
    sends, (turned_ref, tile_ref) = refs[:count], refs[count:]
    reach = 7
    b = lax.axis_index("bulk")
    groups = ny // ROWS
    extent = (zb + 2 * reach) * ROWS
    edge = jnp.zeros((reach * ROWS, LANES), jnp.float32)
    turned_ref[: reach * ROWS] = edge
    turned_ref[(reach + nx) * ROWS :] = edge
    for tile in range(nx // LANES):
        if nx > LANES:
            tile_ref[...] = image_ref[:, tile * LANES : (tile + 1) * LANES]
            source = tile_ref
        else:
            source = image_ref
        for low in range(ROWS):
            pieces = [
                source[pl.ds(ROWS * group + low, zb, stride=ny), :] for group in range(groups)
            ]
            block = jnp.concatenate(pieces, axis=0).T
            turned_ref[pl.ds((tile * LANES + reach) * ROWS + low, LANES, stride=ROWS), :] = block
    for k in range(count):
        start = jnp.bitwise_xor(b, k) * (zb * ROWS)
        sends[k][...] = turned_ref[pl.ds(pl.multiple_of(start, ROWS), extent), :]


def forward_kernel(zb, ny, nx, planes, scalar_ref, taps_ref, visible_ref, estimate_ref, near_ref,
                   other_ref, inverse_ref, rows_high_ref, rows_low_ref, lanes_ref,
                   weight_ref, splat_ref, flag_ref,
                   wide_ref):
    taps = taps_ref.shape[1]
    reach = taps // 2
    moved, core = scalar_ref[0], scalar_ref[1]
    flag_ref[...] = jnp.full((ROWS, LANES), scalar_ref[2], jnp.int32)
    wide_ref[2 * reach : 2 * reach + zb] = estimate_ref[...]
    b, count = lax.axis_index("bulk"), lax.axis_size("bulk")
    above = jnp.bitwise_xor(lax.rem(b, 2), 1 - core)
    for block_ref, side in ((near_ref, above), (other_ref, 1 - above)):
        inside = jnp.logical_and(b + 2 * side - 1 >= 0, b + 2 * side - 1 < count)
        wide_ref[pl.ds((2 * reach + zb) * side, 2 * reach)] = jnp.where(inside, block_ref[...], 0.0)
    rest = planes - zb - 2 * reach
    wide_ref[4 * reach + zb :] = jnp.zeros((rest, ny, nx), jnp.float32)

    rows_high, rows_low = rows_matrix(taps_ref, 1, ny, moved, False)
    lanes = lanes_matrix(taps_ref, 2, nx, False)
    group = WIDE // ny

    tile = (ROWS, LANES)
    splats = [jnp.full(tile, taps_ref[0, t], jnp.float32) for t in range(taps)]
    for t in range(taps):
        splat_ref[taps - 1 - t] = splats[t]
    for base in range(0, planes, group):
        values = blur_planes(wide_ref, splats, base, group)
        values = blur_lanes(lanes, blur_rows(rows_high, rows_low, values))
        inverse_ref[base : base + group] = (1.0 / values).reshape(group, ny, nx)
    high, low = rows_matrix(taps_ref, 1, ny, moved, True)
    rows_high_ref[...] = high
    rows_low_ref[...] = low
    lanes_ref[...] = lanes_matrix(taps_ref, 2, nx, True)
    for plane in range(zb):
        weight = jnp.where(visible_ref[plane] == 1, 1.0, 0.0)
        weight_ref[plane] = jnp.full((ROWS, LANES), weight, jnp.float32)


def neighbours(count):
    return [k for k in range(1, count) if k & (k + 1) == 0]


def beside_in(b, k):
    low = jnp.bitwise_and(b, k)
    return jnp.logical_or(low == k // 2, low == k // 2 + 1)


def ratio_kernel(zb, ny, nx, count, flag_ref, weight_ref, splat_ref, image_ref, inverse_ref,
                 rows_high_ref, rows_low_ref, lanes_ref, *refs):
    blocks, (send_ref, keep_ref, ratio_ref, placed_ref) = refs[:count], refs[count:]
    reach = splat_ref.shape[0] // 2
    b = lax.axis_index("bulk")
    groups = ny // ROWS
    planes = zb + 2 * reach
    turned = flag_ref[...] == 1
    for k in range(count):
        placed_ref[jnp.bitwise_xor(b, k)] = blocks[k][: planes * ROWS]
    odd = lax.rem(b, 2) == 1
    spot = lax.broadcasted_iota(jnp.int32, (ROWS, LANES), 1) // zb
    outside = {0: b > 0, reach + zb: b < count - 1}
    for tile in range(nx // LANES):
        lanes = slice(tile * LANES, (tile + 1) * LANES)
        for plane in range(planes):
            place = slice(plane * ROWS, (plane + 1) * ROWS)
            pieces = [placed_ref[groups * tile + c, place] for c in range(groups)]
            for g in range(groups):
                rows = slice(g * ROWS, (g + 1) * ROWS)
                value = None
                for c in range(groups):
                    shift = (zb * (c - g)) % LANES
                    moved = pltpu.roll(pieces[c], shift, 1) if shift else pieces[c]
                    value = moved if value is None else jnp.where(spot == c, moved, value)
                if reach <= plane < reach + zb:
                    start = (plane - reach) * ny + g * ROWS
                    straight = image_ref[start : start + ROWS, lanes]
                else:
                    side = 0 if plane < reach else reach + zb
                    start = (tile * reach + plane - side) * ny + g * ROWS
                    beside = [blocks[k][start : start + ROWS] for k in neighbours(count)]
                    far = beside[1]
                    for k, value2 in zip(neighbours(count)[2:], beside[2:]):
                        far = jnp.where(beside_in(b, k), value2, far)
                    straight = jnp.where(odd == (side == 0), beside[0], far)
                    straight = jnp.where(outside[side], straight, 0.0)
                value = jnp.where(turned, value, straight)
                ratio_ref[plane, rows, lanes] = value * inverse_ref[plane, rows, lanes]

    adjoint_kernel(0, weight_ref, splat_ref, ratio_ref, rows_high_ref, rows_low_ref, lanes_ref,
                   send_ref, keep_ref)


def adjoint_kernel(part, weight_ref, splat_ref, ratio_ref, rows_high_ref, rows_low_ref, lanes_ref,
                   send_ref, keep_ref):
    core = lax.rem(lax.axis_index("view"), 2)
    splats = [splat_ref[t] for t in range(splat_ref.shape[0])]
    rows_high, rows_low, lanes_pair = rows_high_ref[...], rows_low_ref[...], lanes_ref[...]
    size, ny, nx = send_ref.shape
    group = WIDE // ny
    for out_ref, side in ((send_ref, 1 - core), (keep_ref, core)):
        for first in range(0, size, group):
            base = (2 * part + side) * size + first
            values = blur_planes(ratio_ref, splats, base, group)
            values = blur_lanes(lanes_pair, blur_rows(rows_high, rows_low, values))
            logs = jnp.log(values).reshape(group, ny // ROWS, ROWS, nx)
            for plane in range(group):
                weight = weight_ref[base + plane]
                for tile in range(nx // LANES):
                    lanes = slice(tile * LANES, (tile + 1) * LANES)
                    for row in range(ny // ROWS):
                        out_ref[first + plane, row * ROWS : (row + 1) * ROWS, lanes] = (
                            weight * logs[plane, row, :, lanes]
                        )


def shards(estimate, image, psf, perm, shift, visible):
    zb, ny, nx = estimate.shape
    views, count = lax.axis_size("view"), lax.axis_size("bulk")
    view = lax.axis_index("view")
    core, chip = view % 2, view // 2
    taps = psf.shape[2]
    reach = taps // 2
    kernels = psf[0] / jnp.sum(psf[0], axis=1, keepdims=True)
    stack = image[0].reshape(zb * ny, nx)

    tiles = nx // LANES
    halo = reach * ny
    extent = (zb + 2 * reach) * ROWS
    packed = list(pl.pallas_call(
        functools.partial(pack_kernel, zb, ny, nx, count),
        out_shape=[struct((extent, LANES))] * count,
        in_specs=[VMEM],
        out_specs=[VMEM] * count,
        scratch_shapes=[
            pltpu.VMEM(((nx + 2 * reach) * ROWS, LANES), jnp.float32),
            pltpu.VMEM((zb * ny, LANES), jnp.float32),
        ],
        compiler_params=PARAMS,
    )(stack))
    late_perm, _ = lax.optimization_barrier((perm, packed[1]))
    length = max(extent, halo * tiles)

    bulk = lax.axis_index("bulk")
    even = bulk % 2 == 0

    def beside(first):
        planes = lax.dynamic_slice_in_dim(stack, first, halo, 0).reshape(halo, tiles, LANES)
        planes = jnp.swapaxes(planes, 0, 1).reshape(halo * tiles, LANES)
        return jnp.pad(planes, ((0, length - halo * tiles), (0, 0)))

    for k in neighbours(count):
        block = jnp.pad(packed[k], ((0, length - extent), (0, 0)))
        above = even if k == 1 else jnp.logical_not(even)
        start = jnp.where(above, (zb - reach) * ny, 0)
        packed[k] = jnp.where(late_perm[0] == 1, block, beside(start))
    packed[count - 1], _ = lax.optimization_barrier((packed[count - 1], packed[2]))
    blocks = {0: packed[0]}
    for k in range(count - 1, 0, -1):
        blocks[k] = lax.ppermute(packed[k], "bulk", [(i, i ^ k) for i in range(count)])
    blocks = [blocks[k] for k in range(count)]

    joined_taps = jnp.where(late_perm[0] == 1, kernels[::-1], kernels)
    scalars = jnp.stack([shift[0], core.astype(jnp.int32), late_perm[0]])

    swap = [(i, i ^ 1) for i in range(views)]
    later = estimate
    def beside_of(v, i):
        there = i ^ 1 if v % 2 == 0 else ((i + 1) ^ 1) - 1
        return there if 0 <= there < count else i

    start = jnp.where(even == (core == 0), zb - 2 * reach, 0)
    near = lax.ppermute(
        lax.dynamic_slice_in_dim(later, start, 2 * reach, 0),
        ("view", "bulk"),
        [(v * count + i, v * count + beside_of(v, i)) for v in range(views) for i in range(count)],
    )
    other = lax.ppermute(near, "view", swap)

    group = WIDE // ny
    planes = -(-(zb + 2 * reach) // group) * group
    inverse, rows_high, rows_low, lanes_pair, weight, splats, flags = pl.pallas_call(
        functools.partial(forward_kernel, zb, ny, nx, planes),
        out_shape=[
            struct((planes, ny, nx)),
            struct((WIDE, WIDE), jnp.bfloat16),
            struct((WIDE, WIDE), jnp.bfloat16),
            struct((2 * nx, 2 * nx), jnp.bfloat16),
            struct((zb, ROWS, LANES)),
            struct((taps, ROWS, LANES)),
            struct((ROWS, LANES), jnp.int32),
        ],
        in_specs=[SMEM] * 3 + [VMEM] * 3,
        out_specs=[VMEM] * 7,
        scratch_shapes=[pltpu.VMEM((planes + 2 * reach, ny, nx), jnp.float32)],
        compiler_params=PARAMS,
    )(scalars, joined_taps, visible[0], estimate, near, other)

    parts = 2
    size = zb // (2 * parts)
    matrices = (rows_high, rows_low, lanes_pair)
    first = pl.pallas_call(
        functools.partial(ratio_kernel, zb, ny, nx, count),
        out_shape=[struct((size, ny, nx))] * 2 + [struct((zb + 2 * reach, ny, nx))],
        in_specs=[VMEM] * (8 + count),
        out_specs=[VMEM] * 3,
        scratch_shapes=[
            pltpu.VMEM((count, (zb + 2 * reach) * ROWS, LANES), jnp.float32),
        ],
        compiler_params=PARAMS,
    )(flags, weight, splats, stack, inverse, *matrices, *blocks)
    total = [first[1] + lax.ppermute(first[0], "view", swap)]
    for part in range(1, parts):
        held = weight
        send, keep = pl.pallas_call(
            functools.partial(adjoint_kernel, part),
            out_shape=[struct((size, ny, nx))] * 2,
            in_specs=[VMEM] * 6,
            out_specs=[VMEM] * 2,
            cost_estimate=COST,
            compiler_params=PARAMS,
        )(held, splats, first[2], *matrices)
        total.append(keep + lax.ppermute(send, "view", swap))

    bits = (views // 2).bit_length() - 1
    result = []
    for part in range(parts):
        for step in range(bits):
            flips = [2 << step, 2 << ((step + bits - 1) % bits)]
            total[part] = total[part] + lax.ppermute(
                total[part], "view", [(i, i ^ flips[i % 2]) for i in range(views)]
            )
        held = estimate if not part else lax.optimization_barrier((estimate, own))[0]
        own = lax.dynamic_slice_in_dim(held, (2 * part + core) * size, size, 0)
        own = own * jnp.exp(total[part] / float(views))
        their = lax.ppermute(own, "view", swap)
        result += [jnp.where(core == 0, own, their), jnp.where(core == 0, their, own)]
    return jnp.concatenate(result, axis=0)


def solution(mesh):
    placed = (
        P("bulk", None, None),
        P("view", "bulk", None, None),
        P("view", None, None),
        P("view"),
        P("view"),
        P("view", "bulk"),
    )
    return jax.shard_map(
        shards, mesh=mesh, in_specs=placed, out_specs=P("bulk", None, None), check_vma=False
    )
```

```python
import functools

import jax
import jax.numpy as jnp
from jax import lax
from jax.experimental import pallas as pl
from jax.experimental.pallas import tpu as pltpu
from jax.sharding import PartitionSpec as P

LANES = 128
ROWS = 8
WIDE = 256
VMEM = pl.BlockSpec(memory_space=pltpu.VMEM)
SMEM = pl.BlockSpec(memory_space=pltpu.SMEM)
COST = pl.CostEstimate(flops=2**29, bytes_accessed=2**21, transcendentals=2**16)
PARAMS = pltpu.CompilerParams(vmem_limit_bytes=40 * 1024 * 1024)


def struct(shape, dtype=jnp.float32):
    return jax.ShapeDtypeStruct(shape, dtype)


def halves(values):
    high = values.astype(jnp.bfloat16)
    low = (values - high.astype(jnp.float32)).astype(jnp.bfloat16)
    return high, low


def dot(left, right):
    return jnp.dot(left, right, preferred_element_type=jnp.float32)


def blur_rows(left_high, left_low, values):
    width = values.shape[1]
    high, low = halves(values)
    both = dot(left_high, jnp.concatenate([high, low], axis=1))
    return both[:, :width] + both[:, width:] + dot(left_low, high)


def blur_lanes(right, values):
    width = values.shape[1]
    out = dot(jnp.concatenate(halves(values), axis=1), right)
    return out[:, :width] + out[:, width:]


def lanes_matrix(taps_ref, row, extent, adjoint):
    taps = taps_ref.shape[1]
    source = lax.broadcasted_iota(jnp.int32, (extent, extent), 0)
    target = lax.broadcasted_iota(jnp.int32, (extent, extent), 1)
    offset = (target - source if adjoint else source - target) + taps // 2
    matrix = jnp.zeros((extent, extent), jnp.float32)
    for t in range(taps):
        matrix = jnp.where(offset == t, taps_ref[row, t], matrix)
    high, low = halves(matrix)
    pair = jnp.concatenate([high, low], axis=1)
    return jnp.concatenate([pair, pair], axis=0)


def rows_matrix(taps_ref, row, period, moved, adjoint):
    taps = taps_ref.shape[1]
    target = lax.broadcasted_iota(jnp.int32, (period, WIDE), 0)
    source = lax.broadcasted_iota(jnp.int32, (period, WIDE), 1)
    ahead = target - source if adjoint else source - target
    offset = jnp.bitwise_and(ahead + taps // 2 + moved, period - 1)
    block = jnp.zeros((period, WIDE), jnp.float32)
    for t in range(taps):
        block = jnp.where(offset == t, taps_ref[row, t], block)
    plane = source // period
    return halves(
        jnp.concatenate([jnp.where(plane == p, block, 0.0) for p in range(WIDE // period)], axis=0)
    )


def blur_planes(source_ref, splats, base, group):
    ny, nx = source_ref.shape[1:]
    taps = len(splats)
    columns = []
    for tile in range(nx // LANES):
        lanes = slice(tile * LANES, (tile + 1) * LANES)
        places = []
        for row in range(ny // ROWS):
            rows = slice(row * ROWS, (row + 1) * ROWS)
            source = [source_ref[base + i, rows, lanes] for i in range(group + taps - 1)]
            sums = []
            for plane in range(group):
                total = splats[0] * source[plane]
                for t in range(1, taps):
                    total = total + splats[t] * source[plane + t]
                sums.append(total)
            places.append(sums)
        columns.append(
            jnp.concatenate([sums[plane] for plane in range(group) for sums in places], axis=0)
        )
    return columns[0] if len(columns) == 1 else jnp.concatenate(columns, axis=1)


def pack_kernel(zb, ny, nx, count, image_ref, *refs):
    sends, (turned_ref, tile_ref) = refs[:count], refs[count:]
    reach = 7
    b = lax.axis_index("bulk")
    groups = ny // ROWS
    extent = (zb + 2 * reach) * ROWS
    edge = jnp.zeros((reach * ROWS, LANES), jnp.float32)
    turned_ref[: reach * ROWS] = edge
    turned_ref[(reach + nx) * ROWS :] = edge
    for tile in range(nx // LANES):
        if nx > LANES:
            tile_ref[...] = image_ref[:, tile * LANES : (tile + 1) * LANES]
            source = tile_ref
        else:
            source = image_ref
        for low in range(ROWS):
            pieces = [
                source[pl.ds(ROWS * group + low, zb, stride=ny), :] for group in range(groups)
            ]
            block = jnp.concatenate(pieces, axis=0).T
            turned_ref[pl.ds((tile * LANES + reach) * ROWS + low, LANES, stride=ROWS), :] = block
    for k in range(count):
        start = jnp.bitwise_xor(b, k) * (zb * ROWS)
        sends[k][...] = turned_ref[pl.ds(pl.multiple_of(start, ROWS), extent), :]


def forward_kernel(zb, ny, nx, planes, scalar_ref, taps_ref, visible_ref, estimate_ref, near_ref,
                   other_ref, inverse_ref, rows_high_ref, rows_low_ref, lanes_ref,
                   weight_ref, splat_ref, flag_ref,
                   wide_ref):
    taps = taps_ref.shape[1]
    reach = taps // 2
    moved, core = scalar_ref[0], scalar_ref[1]
    flag_ref[...] = jnp.full((ROWS, LANES), scalar_ref[2], jnp.int32)
    wide_ref[2 * reach : 2 * reach + zb] = estimate_ref[...]
    b, count = lax.axis_index("bulk"), lax.axis_size("bulk")
    above = jnp.bitwise_xor(lax.rem(b, 2), 1 - core)
    for block_ref, side in ((near_ref, above), (other_ref, 1 - above)):
        inside = jnp.logical_and(b + 2 * side - 1 >= 0, b + 2 * side - 1 < count)
        wide_ref[pl.ds((2 * reach + zb) * side, 2 * reach)] = jnp.where(inside, block_ref[...], 0.0)
    rest = planes - zb - 2 * reach
    wide_ref[4 * reach + zb :] = jnp.zeros((rest, ny, nx), jnp.float32)

    rows_high, rows_low = rows_matrix(taps_ref, 1, ny, moved, False)
    lanes = lanes_matrix(taps_ref, 2, nx, False)
    group = WIDE // ny

    tile = (ROWS, LANES)
    splats = [jnp.full(tile, taps_ref[0, t], jnp.float32) for t in range(taps)]
    for t in range(taps):
        splat_ref[taps - 1 - t] = splats[t]
    for base in range(0, planes, group):
        values = blur_planes(wide_ref, splats, base, group)
        values = blur_lanes(lanes, blur_rows(rows_high, rows_low, values))
        inverse_ref[base : base + group] = (1.0 / values).reshape(group, ny, nx)
    high, low = rows_matrix(taps_ref, 1, ny, moved, True)
    rows_high_ref[...] = high
    rows_low_ref[...] = low
    lanes_ref[...] = lanes_matrix(taps_ref, 2, nx, True)
    for plane in range(zb):
        weight = jnp.where(visible_ref[plane] == 1, 1.0, 0.0)
        weight_ref[plane] = jnp.full((ROWS, LANES), weight, jnp.float32)


def neighbours(count):
    return [k for k in range(1, count) if k & (k + 1) == 0]


def beside_in(b, k):
    low = jnp.bitwise_and(b, k)
    return jnp.logical_or(low == k // 2, low == k // 2 + 1)


def ratio_kernel(zb, ny, nx, count, flag_ref, weight_ref, splat_ref, image_ref, inverse_ref,
                 rows_high_ref, rows_low_ref, lanes_ref, *refs):
    blocks, (send_ref, keep_ref, ratio_ref, placed_ref) = refs[:count], refs[count:]
    reach = splat_ref.shape[0] // 2
    b = lax.axis_index("bulk")
    groups = ny // ROWS
    planes = zb + 2 * reach
    turned = flag_ref[...] == 1
    for k in range(count):
        placed_ref[jnp.bitwise_xor(b, k)] = blocks[k][: planes * ROWS]
    odd = lax.rem(b, 2) == 1
    spot = lax.broadcasted_iota(jnp.int32, (ROWS, LANES), 1) // zb
    outside = {0: b > 0, reach + zb: b < count - 1}
    for tile in range(nx // LANES):
        lanes = slice(tile * LANES, (tile + 1) * LANES)
        for plane in range(planes):
            place = slice(plane * ROWS, (plane + 1) * ROWS)
            pieces = [placed_ref[groups * tile + c, place] for c in range(groups)]
            for g in range(groups):
                rows = slice(g * ROWS, (g + 1) * ROWS)
                value = None
                for c in range(groups):
                    shift = (zb * (c - g)) % LANES
                    moved = pltpu.roll(pieces[c], shift, 1) if shift else pieces[c]
                    value = moved if value is None else jnp.where(spot == c, moved, value)
                if reach <= plane < reach + zb:
                    start = (plane - reach) * ny + g * ROWS
                    straight = image_ref[start : start + ROWS, lanes]
                else:
                    side = 0 if plane < reach else reach + zb
                    start = (tile * reach + plane - side) * ny + g * ROWS
                    beside = [blocks[k][start : start + ROWS] for k in neighbours(count)]
                    far = beside[1]
                    for k, value2 in zip(neighbours(count)[2:], beside[2:]):
                        far = jnp.where(beside_in(b, k), value2, far)
                    straight = jnp.where(odd == (side == 0), beside[0], far)
                    straight = jnp.where(outside[side], straight, 0.0)
                value = jnp.where(turned, value, straight)
                ratio_ref[plane, rows, lanes] = value * inverse_ref[plane, rows, lanes]

    adjoint_kernel(0, weight_ref, splat_ref, ratio_ref, rows_high_ref, rows_low_ref, lanes_ref,
                   send_ref, keep_ref)


def adjoint_kernel(part, weight_ref, splat_ref, ratio_ref, rows_high_ref, rows_low_ref, lanes_ref,
                   send_ref, keep_ref):
    core = lax.rem(lax.axis_index("view"), 2)
    splats = [splat_ref[t] for t in range(splat_ref.shape[0])]
    rows_high, rows_low, lanes_pair = rows_high_ref[...], rows_low_ref[...], lanes_ref[...]
    size, ny, nx = send_ref.shape
    group = WIDE // ny
    for out_ref, side in ((send_ref, 1 - core), (keep_ref, core)):
        for first in range(0, size, group):
            base = (2 * part + side) * size + first
            values = blur_planes(ratio_ref, splats, base, group)
            values = blur_lanes(lanes_pair, blur_rows(rows_high, rows_low, values))
            logs = jnp.log(values).reshape(group, ny // ROWS, ROWS, nx)
            for plane in range(group):
                weight = weight_ref[base + plane]
                for tile in range(nx // LANES):
                    lanes = slice(tile * LANES, (tile + 1) * LANES)
                    for row in range(ny // ROWS):
                        out_ref[first + plane, row * ROWS : (row + 1) * ROWS, lanes] = (
                            weight * logs[plane, row, :, lanes]
                        )


def shards(estimate, image, psf, perm, shift, visible):
    zb, ny, nx = estimate.shape
    views, count = lax.axis_size("view"), lax.axis_size("bulk")
    view = lax.axis_index("view")
    core, chip = view % 2, view // 2
    taps = psf.shape[2]
    reach = taps // 2
    kernels = psf[0] / jnp.sum(psf[0], axis=1, keepdims=True)
    stack = image[0].reshape(zb * ny, nx)

    tiles = nx // LANES
    halo = reach * ny
    extent = (zb + 2 * reach) * ROWS
    packed = list(pl.pallas_call(
        functools.partial(pack_kernel, zb, ny, nx, count),
        out_shape=[struct((extent, LANES))] * count,
        in_specs=[VMEM],
        out_specs=[VMEM] * count,
        scratch_shapes=[
            pltpu.VMEM(((nx + 2 * reach) * ROWS, LANES), jnp.float32),
            pltpu.VMEM((zb * ny, LANES), jnp.float32),
        ],
        compiler_params=PARAMS,
    )(stack))
    late_perm, _ = lax.optimization_barrier((perm, packed[1]))
    length = max(extent, halo * tiles)

    bulk = lax.axis_index("bulk")
    even = bulk % 2 == 0

    def beside(first):
        planes = lax.dynamic_slice_in_dim(stack, first, halo, 0).reshape(halo, tiles, LANES)
        planes = jnp.swapaxes(planes, 0, 1).reshape(halo * tiles, LANES)
        return jnp.pad(planes, ((0, length - halo * tiles), (0, 0)))

    for k in neighbours(count):
        block = jnp.pad(packed[k], ((0, length - extent), (0, 0)))
        above = even if k == 1 else jnp.logical_not(even)
        start = jnp.where(above, (zb - reach) * ny, 0)
        packed[k] = jnp.where(late_perm[0] == 1, block, beside(start))
    packed[count - 1], _ = lax.optimization_barrier((packed[count - 1], packed[2]))
    blocks = {0: packed[0]}
    for k in range(count - 1, 0, -1):
        blocks[k] = lax.ppermute(packed[k], "bulk", [(i, i ^ k) for i in range(count)])
    blocks = [blocks[k] for k in range(count)]

    joined_taps = jnp.where(late_perm[0] == 1, kernels[::-1], kernels)
    scalars = jnp.stack([shift[0], core.astype(jnp.int32), late_perm[0]])

    swap = [(i, i ^ 1) for i in range(views)]
    def beside_of(v, i):
        there = i ^ 1 if v % 2 == 0 else ((i + 1) ^ 1) - 1
        return there if 0 <= there < count else i

    side = chip % 2
    start = jnp.where(even == (core == 0), zb - 2 * reach, 0) + reach * side
    quarter = lax.ppermute(
        lax.dynamic_slice_in_dim(estimate, start, reach, 0),
        ("view", "bulk"),
        [(v * count + i, v * count + beside_of(v, i)) for v in range(views) for i in range(count)],
    )
    across = lax.ppermute(quarter, "view", [(v, v ^ 2) for v in range(views)])
    near = jnp.concatenate([
        jnp.where(side == 0, quarter, across), jnp.where(side == 0, across, quarter)
    ])
    other = lax.ppermute(near, "view", swap)

    group = WIDE // ny
    planes = -(-(zb + 2 * reach) // group) * group
    inverse, rows_high, rows_low, lanes_pair, weight, splats, flags = pl.pallas_call(
        functools.partial(forward_kernel, zb, ny, nx, planes),
        out_shape=[
            struct((planes, ny, nx)),
            struct((WIDE, WIDE), jnp.bfloat16),
            struct((WIDE, WIDE), jnp.bfloat16),
            struct((2 * nx, 2 * nx), jnp.bfloat16),
            struct((zb, ROWS, LANES)),
            struct((taps, ROWS, LANES)),
            struct((ROWS, LANES), jnp.int32),
        ],
        in_specs=[SMEM] * 3 + [VMEM] * 3,
        out_specs=[VMEM] * 7,
        scratch_shapes=[pltpu.VMEM((planes + 2 * reach, ny, nx), jnp.float32)],
        compiler_params=PARAMS,
    )(scalars, joined_taps, visible[0], estimate, near, other)

    parts = 2
    size = zb // (2 * parts)
    matrices = (rows_high, rows_low, lanes_pair)
    first = pl.pallas_call(
        functools.partial(ratio_kernel, zb, ny, nx, count),
        out_shape=[struct((size, ny, nx))] * 2 + [struct((zb + 2 * reach, ny, nx))],
        in_specs=[VMEM] * (8 + count),
        out_specs=[VMEM] * 3,
        scratch_shapes=[
            pltpu.VMEM((count, (zb + 2 * reach) * ROWS, LANES), jnp.float32),
        ],
        compiler_params=PARAMS,
    )(flags, weight, splats, stack, inverse, *matrices, *blocks)
    total = [first[1] + lax.ppermute(first[0], "view", swap)]
    for part in range(1, parts):
        held = weight
        send, keep = pl.pallas_call(
            functools.partial(adjoint_kernel, part),
            out_shape=[struct((size, ny, nx))] * 2,
            in_specs=[VMEM] * 6,
            out_specs=[VMEM] * 2,
            cost_estimate=COST,
            compiler_params=PARAMS,
        )(held, splats, first[2], *matrices)
        total.append(keep + lax.ppermute(send, "view", swap))

    bits = (views // 2).bit_length() - 1
    result = []
    for part in range(parts):
        for step in range(bits):
            flips = [2 << step, 2 << ((step + bits - 1) % bits)]
            total[part] = total[part] + lax.ppermute(
                total[part], "view", [(i, i ^ flips[i % 2]) for i in range(views)]
            )
        held = estimate if not part else lax.optimization_barrier((estimate, own))[0]
        own = lax.dynamic_slice_in_dim(held, (2 * part + core) * size, size, 0)
        own = own * jnp.exp(total[part] / float(views))
        their = lax.ppermute(own, "view", swap)
        result += [jnp.where(core == 0, own, their), jnp.where(core == 0, their, own)]
    return jnp.concatenate(result, axis=0)


def solution(mesh):
    placed = (
        P("bulk", None, None),
        P("view", "bulk", None, None),
        P("view", None, None),
        P("view"),
        P("view"),
        P("view", "bulk"),
    )
    return jax.shard_map(
        shards, mesh=mesh, in_specs=placed, out_specs=P("bulk", None, None), check_vma=False
    )
```

```python
import functools

import jax
import jax.numpy as jnp
from jax import lax
from jax.experimental import pallas as pl
from jax.experimental.pallas import tpu as pltpu
from jax.sharding import PartitionSpec as P

LANES = 128
ROWS = 8
WIDE = 256
VMEM = pl.BlockSpec(memory_space=pltpu.VMEM)
SMEM = pl.BlockSpec(memory_space=pltpu.SMEM)
COST = pl.CostEstimate(flops=2**29, bytes_accessed=2**21, transcendentals=2**16)
PARAMS = pltpu.CompilerParams(vmem_limit_bytes=40 * 1024 * 1024)


def struct(shape, dtype=jnp.float32):
    return jax.ShapeDtypeStruct(shape, dtype)


def halves(values):
    high = values.astype(jnp.bfloat16)
    low = (values - high.astype(jnp.float32)).astype(jnp.bfloat16)
    return high, low


def dot(left, right):
    return jnp.dot(left, right, preferred_element_type=jnp.float32)


def blur_rows(left_high, left_low, values):
    width = values.shape[1]
    high, low = halves(values)
    both = dot(left_high, jnp.concatenate([high, low], axis=1))
    return both[:, :width] + both[:, width:] + dot(left_low, high)


def blur_lanes(right, values):
    width = values.shape[1]
    out = dot(jnp.concatenate(halves(values), axis=1), right)
    return out[:, :width] + out[:, width:]


def lanes_matrix(taps_ref, row, extent, adjoint):
    taps = taps_ref.shape[1]
    source = lax.broadcasted_iota(jnp.int32, (extent, extent), 0)
    target = lax.broadcasted_iota(jnp.int32, (extent, extent), 1)
    offset = (target - source if adjoint else source - target) + taps // 2
    matrix = jnp.zeros((extent, extent), jnp.float32)
    for t in range(taps):
        matrix = jnp.where(offset == t, taps_ref[row, t], matrix)
    high, low = halves(matrix)
    pair = jnp.concatenate([high, low], axis=1)
    return jnp.concatenate([pair, pair], axis=0)


def rows_matrix(taps_ref, row, period, moved, adjoint):
    taps = taps_ref.shape[1]
    target = lax.broadcasted_iota(jnp.int32, (period, WIDE), 0)
    source = lax.broadcasted_iota(jnp.int32, (period, WIDE), 1)
    ahead = target - source if adjoint else source - target
    offset = jnp.bitwise_and(ahead + taps // 2 + moved, period - 1)
    block = jnp.zeros((period, WIDE), jnp.float32)
    for t in range(taps):
        block = jnp.where(offset == t, taps_ref[row, t], block)
    plane = source // period
    return halves(
        jnp.concatenate([jnp.where(plane == p, block, 0.0) for p in range(WIDE // period)], axis=0)
    )


def blur_planes(source_ref, splats, base, group):
    ny, nx = source_ref.shape[1:]
    taps = len(splats)
    columns = []
    for tile in range(nx // LANES):
        lanes = slice(tile * LANES, (tile + 1) * LANES)
        places = []
        for row in range(ny // ROWS):
            rows = slice(row * ROWS, (row + 1) * ROWS)
            source = [source_ref[base + i, rows, lanes] for i in range(group + taps - 1)]
            sums = []
            for plane in range(group):
                total = splats[0] * source[plane]
                for t in range(1, taps):
                    total = total + splats[t] * source[plane + t]
                sums.append(total)
            places.append(sums)
        columns.append(
            jnp.concatenate([sums[plane] for plane in range(group) for sums in places], axis=0)
        )
    return columns[0] if len(columns) == 1 else jnp.concatenate(columns, axis=1)


def pack_kernel(zb, ny, nx, count, image_ref, *refs):
    sends, (turned_ref, tile_ref) = refs[:count], refs[count:]
    reach = 7
    b = lax.axis_index("bulk")
    groups = ny // ROWS
    extent = (zb + 2 * reach) * ROWS
    edge = jnp.zeros((reach * ROWS, LANES), jnp.float32)
    turned_ref[: reach * ROWS] = edge
    turned_ref[(reach + nx) * ROWS :] = edge
    for tile in range(nx // LANES):
        if nx > LANES:
            tile_ref[...] = image_ref[:, tile * LANES : (tile + 1) * LANES]
            source = tile_ref
        else:
            source = image_ref
        for low in range(ROWS):
            pieces = [
                source[pl.ds(ROWS * group + low, zb, stride=ny), :] for group in range(groups)
            ]
            block = jnp.concatenate(pieces, axis=0).T
            turned_ref[pl.ds((tile * LANES + reach) * ROWS + low, LANES, stride=ROWS), :] = block
    for k in range(count):
        start = jnp.bitwise_xor(b, k) * (zb * ROWS)
        sends[k][...] = turned_ref[pl.ds(pl.multiple_of(start, ROWS), extent), :]


def forward_kernel(zb, ny, nx, planes, scalar_ref, taps_ref, visible_ref, estimate_ref, near_ref,
                   other_ref, inverse_ref, rows_high_ref, rows_low_ref, lanes_ref,
                   weight_ref, splat_ref, flag_ref,
                   wide_ref):
    taps = taps_ref.shape[1]
    reach = taps // 2
    moved, core = scalar_ref[0], scalar_ref[1]
    flag_ref[...] = jnp.full((ROWS, LANES), scalar_ref[2], jnp.int32)
    wide_ref[2 * reach : 2 * reach + zb] = estimate_ref[...]
    b, count = lax.axis_index("bulk"), lax.axis_size("bulk")
    above = jnp.bitwise_xor(lax.rem(b, 2), 1 - core)
    for block_ref, side in ((near_ref, above), (other_ref, 1 - above)):
        inside = jnp.logical_and(b + 2 * side - 1 >= 0, b + 2 * side - 1 < count)
        wide_ref[pl.ds((2 * reach + zb) * side, 2 * reach)] = jnp.where(inside, block_ref[...], 0.0)
    rest = planes - zb - 2 * reach
    wide_ref[4 * reach + zb :] = jnp.zeros((rest, ny, nx), jnp.float32)

    rows_high, rows_low = rows_matrix(taps_ref, 1, ny, moved, False)
    lanes = lanes_matrix(taps_ref, 2, nx, False)
    group = WIDE // ny

    tile = (ROWS, LANES)
    splats = [jnp.full(tile, taps_ref[0, t], jnp.float32) for t in range(taps)]
    for t in range(taps):
        splat_ref[taps - 1 - t] = splats[t]
    for base in range(0, planes, group):
        values = blur_planes(wide_ref, splats, base, group)
        values = blur_lanes(lanes, blur_rows(rows_high, rows_low, values))
        inverse_ref[base : base + group] = (1.0 / values).reshape(group, ny, nx)
    high, low = rows_matrix(taps_ref, 1, ny, moved, True)
    rows_high_ref[...] = high
    rows_low_ref[...] = low
    lanes_ref[...] = lanes_matrix(taps_ref, 2, nx, True)
    for plane in range(zb):
        weight = jnp.where(visible_ref[plane] == 1, 1.0, 0.0)
        weight_ref[plane] = jnp.full((ROWS, LANES), weight, jnp.float32)


def neighbours(count):
    return [k for k in range(1, count) if k & (k + 1) == 0]


def beside_in(b, k):
    low = jnp.bitwise_and(b, k)
    return jnp.logical_or(low == k // 2, low == k // 2 + 1)


def ratio_kernel(zb, ny, nx, count, flag_ref, weight_ref, splat_ref, image_ref, inverse_ref,
                 rows_high_ref, rows_low_ref, lanes_ref, *refs):
    blocks, (send_ref, keep_ref, ratio_ref, placed_ref) = refs[:count], refs[count:]
    reach = splat_ref.shape[0] // 2
    b = lax.axis_index("bulk")
    groups = ny // ROWS
    planes = zb + 2 * reach
    turned = flag_ref[...] == 1
    for k in range(count):
        placed_ref[jnp.bitwise_xor(b, k)] = blocks[k][: planes * ROWS]
    odd = lax.rem(b, 2) == 1
    spot = lax.broadcasted_iota(jnp.int32, (ROWS, LANES), 1) // zb
    outside = {0: b > 0, reach + zb: b < count - 1}
    for tile in range(nx // LANES):
        lanes = slice(tile * LANES, (tile + 1) * LANES)
        for plane in range(planes):
            place = slice(plane * ROWS, (plane + 1) * ROWS)
            pieces = [placed_ref[groups * tile + c, place] for c in range(groups)]
            for g in range(groups):
                rows = slice(g * ROWS, (g + 1) * ROWS)
                value = None
                for c in range(groups):
                    shift = (zb * (c - g)) % LANES
                    moved = pltpu.roll(pieces[c], shift, 1) if shift else pieces[c]
                    value = moved if value is None else jnp.where(spot == c, moved, value)
                if reach <= plane < reach + zb:
                    start = (plane - reach) * ny + g * ROWS
                    straight = image_ref[start : start + ROWS, lanes]
                else:
                    side = 0 if plane < reach else reach + zb
                    start = (tile * reach + plane - side) * ny + g * ROWS
                    beside = [blocks[k][start : start + ROWS] for k in neighbours(count)]
                    far = beside[1]
                    for k, value2 in zip(neighbours(count)[2:], beside[2:]):
                        far = jnp.where(beside_in(b, k), value2, far)
                    straight = jnp.where(odd == (side == 0), beside[0], far)
                    straight = jnp.where(outside[side], straight, 0.0)
                value = jnp.where(turned, value, straight)
                ratio_ref[plane, rows, lanes] = value * inverse_ref[plane, rows, lanes]

    adjoint_kernel(0, weight_ref, splat_ref, ratio_ref, rows_high_ref, rows_low_ref, lanes_ref,
                   send_ref, keep_ref)


def adjoint_kernel(part, weight_ref, splat_ref, ratio_ref, rows_high_ref, rows_low_ref, lanes_ref,
                   send_ref, keep_ref):
    core = lax.rem(lax.axis_index("view"), 2)
    splats = [splat_ref[t] for t in range(splat_ref.shape[0])]
    rows_high, rows_low, lanes_pair = rows_high_ref[...], rows_low_ref[...], lanes_ref[...]
    size, ny, nx = send_ref.shape
    group = WIDE // ny
    for out_ref, side in ((send_ref, 1 - core), (keep_ref, core)):
        for first in range(0, size, group):
            base = (2 * part + side) * size + first
            values = blur_planes(ratio_ref, splats, base, group)
            values = blur_lanes(lanes_pair, blur_rows(rows_high, rows_low, values))
            logs = jnp.log(values).reshape(group, ny // ROWS, ROWS, nx)
            for plane in range(group):
                weight = weight_ref[base + plane]
                for tile in range(nx // LANES):
                    lanes = slice(tile * LANES, (tile + 1) * LANES)
                    for row in range(ny // ROWS):
                        out_ref[first + plane, row * ROWS : (row + 1) * ROWS, lanes] = (
                            weight * logs[plane, row, :, lanes]
                        )


def shards(estimate, image, psf, perm, shift, visible):
    zb, ny, nx = estimate.shape
    views, count = lax.axis_size("view"), lax.axis_size("bulk")
    view = lax.axis_index("view")
    core, chip = view % 2, view // 2
    taps = psf.shape[2]
    reach = taps // 2
    kernels = psf[0] / jnp.sum(psf[0], axis=1, keepdims=True)
    stack = image[0].reshape(zb * ny, nx)

    tiles = nx // LANES
    halo = reach * ny
    extent = (zb + 2 * reach) * ROWS
    packed = list(pl.pallas_call(
        functools.partial(pack_kernel, zb, ny, nx, count),
        out_shape=[struct((extent, LANES))] * count,
        in_specs=[VMEM],
        out_specs=[VMEM] * count,
        scratch_shapes=[
            pltpu.VMEM(((nx + 2 * reach) * ROWS, LANES), jnp.float32),
            pltpu.VMEM((zb * ny, LANES), jnp.float32),
        ],
        compiler_params=PARAMS,
    )(stack))
    late_perm, _ = lax.optimization_barrier((perm, packed[1]))
    length = max(extent, halo * tiles)

    bulk = lax.axis_index("bulk")
    even = bulk % 2 == 0

    def beside(first):
        planes = lax.dynamic_slice_in_dim(stack, first, halo, 0).reshape(halo, tiles, LANES)
        planes = jnp.swapaxes(planes, 0, 1).reshape(halo * tiles, LANES)
        return jnp.pad(planes, ((0, length - halo * tiles), (0, 0)))

    for k in neighbours(count):
        block = jnp.pad(packed[k], ((0, length - extent), (0, 0)))
        above = even if k == 1 else jnp.logical_not(even)
        start = jnp.where(above, (zb - reach) * ny, 0)
        packed[k] = jnp.where(late_perm[0] == 1, block, beside(start))
    packed[1], _ = lax.optimization_barrier((packed[1], packed[2]))
    blocks = {0: packed[0]}
    for k in range(count - 1, 0, -1):
        blocks[k] = lax.ppermute(packed[k], "bulk", [(i, i ^ k) for i in range(count)])
    blocks = [blocks[k] for k in range(count)]

    joined_taps = jnp.where(late_perm[0] == 1, kernels[::-1], kernels)
    scalars = jnp.stack([shift[0], core.astype(jnp.int32), late_perm[0]])

    swap = [(i, i ^ 1) for i in range(views)]
    def beside_of(v, i):
        there = i ^ 1 if v % 2 == 0 else ((i + 1) ^ 1) - 1
        return there if 0 <= there < count else i

    side = chip % 2
    start = jnp.where(even == (core == 0), zb - 2 * reach, 0) + reach * side
    quarter = lax.ppermute(
        lax.dynamic_slice_in_dim(estimate, start, reach, 0),
        ("view", "bulk"),
        [(v * count + i, v * count + beside_of(v, i)) for v in range(views) for i in range(count)],
    )
    across = lax.ppermute(quarter, "view", [(v, v ^ 2) for v in range(views)])
    near = jnp.concatenate([
        jnp.where(side == 0, quarter, across), jnp.where(side == 0, across, quarter)
    ])
    other = lax.ppermute(near, "view", swap)

    group = WIDE // ny
    planes = -(-(zb + 2 * reach) // group) * group
    inverse, rows_high, rows_low, lanes_pair, weight, splats, flags = pl.pallas_call(
        functools.partial(forward_kernel, zb, ny, nx, planes),
        out_shape=[
            struct((planes, ny, nx)),
            struct((WIDE, WIDE), jnp.bfloat16),
            struct((WIDE, WIDE), jnp.bfloat16),
            struct((2 * nx, 2 * nx), jnp.bfloat16),
            struct((zb, ROWS, LANES)),
            struct((taps, ROWS, LANES)),
            struct((ROWS, LANES), jnp.int32),
        ],
        in_specs=[SMEM] * 3 + [VMEM] * 3,
        out_specs=[VMEM] * 7,
        scratch_shapes=[pltpu.VMEM((planes + 2 * reach, ny, nx), jnp.float32)],
        compiler_params=PARAMS,
    )(scalars, joined_taps, visible[0], estimate, near, other)

    parts = 2
    size = zb // (2 * parts)
    matrices = (rows_high, rows_low, lanes_pair)
    first = pl.pallas_call(
        functools.partial(ratio_kernel, zb, ny, nx, count),
        out_shape=[struct((size, ny, nx))] * 2 + [struct((zb + 2 * reach, ny, nx))],
        in_specs=[VMEM] * (8 + count),
        out_specs=[VMEM] * 3,
        scratch_shapes=[
            pltpu.VMEM((count, (zb + 2 * reach) * ROWS, LANES), jnp.float32),
        ],
        compiler_params=PARAMS,
    )(flags, weight, splats, stack, inverse, *matrices, *blocks)
    total = [first[1] + lax.ppermute(first[0], "view", swap)]
    for part in range(1, parts):
        held = weight
        send, keep = pl.pallas_call(
            functools.partial(adjoint_kernel, part),
            out_shape=[struct((size, ny, nx))] * 2,
            in_specs=[VMEM] * 6,
            out_specs=[VMEM] * 2,
            cost_estimate=COST,
            compiler_params=PARAMS,
        )(held, splats, first[2], *matrices)
        total.append(keep + lax.ppermute(send, "view", swap))

    bits = (views // 2).bit_length() - 1
    result = []
    for part in range(parts):
        for step in range(bits):
            flips = [2 << step, 2 << ((step + bits - 1) % bits)]
            total[part] = total[part] + lax.ppermute(
                total[part], "view", [(i, i ^ flips[i % 2]) for i in range(views)]
            )
        held = estimate if not part else lax.optimization_barrier((estimate, own))[0]
        own = lax.dynamic_slice_in_dim(held, (2 * part + core) * size, size, 0)
        own = own * jnp.exp(total[part] / float(views))
        their = lax.ppermute(own, "view", swap)
        result += [jnp.where(core == 0, own, their), jnp.where(core == 0, their, own)]
    return jnp.concatenate(result, axis=0)


def solution(mesh):
    placed = (
        P("bulk", None, None),
        P("view", "bulk", None, None),
        P("view", None, None),
        P("view"),
        P("view"),
        P("view", "bulk"),
    )
    return jax.shard_map(
        shards, mesh=mesh, in_specs=placed, out_specs=P("bulk", None, None), check_vma=False
    )
```

```python
import functools

import jax
import jax.numpy as jnp
from jax import lax
from jax.experimental import pallas as pl
from jax.experimental.pallas import tpu as pltpu
from jax.sharding import PartitionSpec as P

LANES = 128
ROWS = 8
WIDE = 256
VMEM = pl.BlockSpec(memory_space=pltpu.VMEM)
SMEM = pl.BlockSpec(memory_space=pltpu.SMEM)
COST = pl.CostEstimate(flops=2**29, bytes_accessed=2**23, transcendentals=2**16)
PARAMS = pltpu.CompilerParams(vmem_limit_bytes=40 * 1024 * 1024)


def struct(shape, dtype=jnp.float32):
    return jax.ShapeDtypeStruct(shape, dtype)


def halves(values):
    high = values.astype(jnp.bfloat16)
    low = (values - high.astype(jnp.float32)).astype(jnp.bfloat16)
    return high, low


def dot(left, right):
    return jnp.dot(left, right, preferred_element_type=jnp.float32)


def blur_rows(left_high, left_low, values):
    width = values.shape[1]
    high, low = halves(values)
    both = dot(left_high, jnp.concatenate([high, low], axis=1))
    return both[:, :width] + both[:, width:] + dot(left_low, high)


def blur_lanes(right, values):
    width = values.shape[1]
    out = dot(jnp.concatenate(halves(values), axis=1), right)
    return out[:, :width] + out[:, width:]


def lanes_matrix(taps_ref, row, extent, adjoint):
    taps = taps_ref.shape[1]
    source = lax.broadcasted_iota(jnp.int32, (extent, extent), 0)
    target = lax.broadcasted_iota(jnp.int32, (extent, extent), 1)
    offset = (target - source if adjoint else source - target) + taps // 2
    matrix = jnp.zeros((extent, extent), jnp.float32)
    for t in range(taps):
        matrix = jnp.where(offset == t, taps_ref[row, t], matrix)
    high, low = halves(matrix)
    pair = jnp.concatenate([high, low], axis=1)
    return jnp.concatenate([pair, pair], axis=0)


def rows_matrix(taps_ref, row, period, moved, adjoint):
    taps = taps_ref.shape[1]
    target = lax.broadcasted_iota(jnp.int32, (period, WIDE), 0)
    source = lax.broadcasted_iota(jnp.int32, (period, WIDE), 1)
    ahead = target - source if adjoint else source - target
    offset = jnp.bitwise_and(ahead + taps // 2 + moved, period - 1)
    block = jnp.zeros((period, WIDE), jnp.float32)
    for t in range(taps):
        block = jnp.where(offset == t, taps_ref[row, t], block)
    plane = source // period
    return halves(
        jnp.concatenate([jnp.where(plane == p, block, 0.0) for p in range(WIDE // period)], axis=0)
    )


def blur_planes(source_ref, splats, base, group):
    ny, nx = source_ref.shape[1:]
    taps = len(splats)
    columns = []
    for tile in range(nx // LANES):
        lanes = slice(tile * LANES, (tile + 1) * LANES)
        places = []
        for row in range(ny // ROWS):
            rows = slice(row * ROWS, (row + 1) * ROWS)
            source = [source_ref[base + i, rows, lanes] for i in range(group + taps - 1)]
            sums = []
            for plane in range(group):
                total = splats[0] * source[plane]
                for t in range(1, taps):
                    total = total + splats[t] * source[plane + t]
                sums.append(total)
            places.append(sums)
        columns.append(
            jnp.concatenate([sums[plane] for plane in range(group) for sums in places], axis=0)
        )
    return columns[0] if len(columns) == 1 else jnp.concatenate(columns, axis=1)


def pack_kernel(zb, ny, nx, count, image_ref, *refs):
    sends, (turned_ref, tile_ref) = refs[:count], refs[count:]
    reach = 7
    b = lax.axis_index("bulk")
    groups = ny // ROWS
    extent = (zb + 2 * reach) * ROWS
    edge = jnp.zeros((reach * ROWS, LANES), jnp.float32)
    turned_ref[: reach * ROWS] = edge
    turned_ref[(reach + nx) * ROWS :] = edge
    for tile in range(nx // LANES):
        if nx > LANES:
            tile_ref[...] = image_ref[:, tile * LANES : (tile + 1) * LANES]
            source = tile_ref
        else:
            source = image_ref
        for low in range(ROWS):
            pieces = [
                source[pl.ds(ROWS * group + low, zb, stride=ny), :] for group in range(groups)
            ]
            block = jnp.concatenate(pieces, axis=0).T
            turned_ref[pl.ds((tile * LANES + reach) * ROWS + low, LANES, stride=ROWS), :] = block
    for k in range(count):
        start = jnp.bitwise_xor(b, k) * (zb * ROWS)
        sends[k][...] = turned_ref[pl.ds(pl.multiple_of(start, ROWS), extent), :]


def forward_kernel(zb, ny, nx, planes, scalar_ref, taps_ref, visible_ref, estimate_ref, near_ref,
                   other_ref, inverse_ref, rows_high_ref, rows_low_ref, lanes_ref,
                   weight_ref, splat_ref, flag_ref,
                   wide_ref):
    taps = taps_ref.shape[1]
    reach = taps // 2
    moved, core = scalar_ref[0], scalar_ref[1]
    flag_ref[...] = jnp.full((ROWS, LANES), scalar_ref[2], jnp.int32)
    wide_ref[2 * reach : 2 * reach + zb] = estimate_ref[...]
    b, count = lax.axis_index("bulk"), lax.axis_size("bulk")
    above = jnp.bitwise_xor(lax.rem(b, 2), 1 - core)
    for block_ref, side in ((near_ref, above), (other_ref, 1 - above)):
        inside = jnp.logical_and(b + 2 * side - 1 >= 0, b + 2 * side - 1 < count)
        wide_ref[pl.ds((2 * reach + zb) * side, 2 * reach)] = jnp.where(inside, block_ref[...], 0.0)
    rest = planes - zb - 2 * reach
    wide_ref[4 * reach + zb :] = jnp.zeros((rest, ny, nx), jnp.float32)

    rows_high, rows_low = rows_matrix(taps_ref, 1, ny, moved, False)
    lanes = lanes_matrix(taps_ref, 2, nx, False)
    group = WIDE // ny

    tile = (ROWS, LANES)
    splats = [jnp.full(tile, taps_ref[0, t], jnp.float32) for t in range(taps)]
    for t in range(taps):
        splat_ref[taps - 1 - t] = splats[t]
    for base in range(0, planes, group):
        values = blur_planes(wide_ref, splats, base, group)
        values = blur_lanes(lanes, blur_rows(rows_high, rows_low, values))
        inverse_ref[base : base + group] = (1.0 / values).reshape(group, ny, nx)
    high, low = rows_matrix(taps_ref, 1, ny, moved, True)
    rows_high_ref[...] = high
    rows_low_ref[...] = low
    lanes_ref[...] = lanes_matrix(taps_ref, 2, nx, True)
    for plane in range(zb):
        weight = jnp.where(visible_ref[plane] == 1, 1.0, 0.0)
        weight_ref[plane] = jnp.full((ROWS, LANES), weight, jnp.float32)


def neighbours(count):
    return [k for k in range(1, count) if k & (k + 1) == 0]


def beside_in(b, k):
    low = jnp.bitwise_and(b, k)
    return jnp.logical_or(low == k // 2, low == k // 2 + 1)


def ratio_kernel(zb, ny, nx, count, flag_ref, weight_ref, splat_ref, image_ref, inverse_ref,
                 rows_high_ref, rows_low_ref, lanes_ref, *refs):
    blocks, (send_ref, keep_ref, ratio_ref, placed_ref) = refs[:count], refs[count:]
    reach = splat_ref.shape[0] // 2
    b = lax.axis_index("bulk")
    groups = ny // ROWS
    planes = zb + 2 * reach
    turned = flag_ref[...] == 1
    for k in range(count):
        placed_ref[jnp.bitwise_xor(b, k)] = blocks[k][: planes * ROWS]
    odd = lax.rem(b, 2) == 1
    spot = lax.broadcasted_iota(jnp.int32, (ROWS, LANES), 1) // zb
    outside = {0: b > 0, reach + zb: b < count - 1}
    for tile in range(nx // LANES):
        lanes = slice(tile * LANES, (tile + 1) * LANES)
        for plane in range(planes):
            place = slice(plane * ROWS, (plane + 1) * ROWS)
            pieces = [placed_ref[groups * tile + c, place] for c in range(groups)]
            for g in range(groups):
                rows = slice(g * ROWS, (g + 1) * ROWS)
                value = None
                for c in range(groups):
                    shift = (zb * (c - g)) % LANES
                    moved = pltpu.roll(pieces[c], shift, 1) if shift else pieces[c]
                    value = moved if value is None else jnp.where(spot == c, moved, value)
                if reach <= plane < reach + zb:
                    start = (plane - reach) * ny + g * ROWS
                    straight = image_ref[start : start + ROWS, lanes]
                else:
                    side = 0 if plane < reach else reach + zb
                    start = (tile * reach + plane - side) * ny + g * ROWS
                    beside = [blocks[k][start : start + ROWS] for k in neighbours(count)]
                    far = beside[1]
                    for k, value2 in zip(neighbours(count)[2:], beside[2:]):
                        far = jnp.where(beside_in(b, k), value2, far)
                    straight = jnp.where(odd == (side == 0), beside[0], far)
                    straight = jnp.where(outside[side], straight, 0.0)
                value = jnp.where(turned, value, straight)
                ratio_ref[plane, rows, lanes] = value * inverse_ref[plane, rows, lanes]

    adjoint_kernel(0, weight_ref, splat_ref, ratio_ref, rows_high_ref, rows_low_ref, lanes_ref,
                   send_ref, keep_ref)


def adjoint_kernel(part, weight_ref, splat_ref, ratio_ref, rows_high_ref, rows_low_ref, lanes_ref,
                   send_ref, keep_ref):
    core = lax.rem(lax.axis_index("view"), 2)
    splats = [splat_ref[t] for t in range(splat_ref.shape[0])]
    rows_high, rows_low, lanes_pair = rows_high_ref[...], rows_low_ref[...], lanes_ref[...]
    size, ny, nx = send_ref.shape
    group = WIDE // ny
    for out_ref, side in ((send_ref, 1 - core), (keep_ref, core)):
        for first in range(0, size, group):
            base = (2 * part + side) * size + first
            values = blur_planes(ratio_ref, splats, base, group)
            values = blur_lanes(lanes_pair, blur_rows(rows_high, rows_low, values))
            logs = jnp.log(values).reshape(group, ny // ROWS, ROWS, nx)
            for plane in range(group):
                weight = weight_ref[base + plane]
                for tile in range(nx // LANES):
                    lanes = slice(tile * LANES, (tile + 1) * LANES)
                    for row in range(ny // ROWS):
                        out_ref[first + plane, row * ROWS : (row + 1) * ROWS, lanes] = (
                            weight * logs[plane, row, :, lanes]
                        )


def shards(estimate, image, psf, perm, shift, visible):
    zb, ny, nx = estimate.shape
    views, count = lax.axis_size("view"), lax.axis_size("bulk")
    view = lax.axis_index("view")
    core, chip = view % 2, view // 2
    taps = psf.shape[2]
    reach = taps // 2
    kernels = psf[0] / jnp.sum(psf[0], axis=1, keepdims=True)
    stack = image[0].reshape(zb * ny, nx)

    tiles = nx // LANES
    halo = reach * ny
    extent = (zb + 2 * reach) * ROWS
    packed = list(pl.pallas_call(
        functools.partial(pack_kernel, zb, ny, nx, count),
        out_shape=[struct((extent, LANES))] * count,
        in_specs=[VMEM],
        out_specs=[VMEM] * count,
        scratch_shapes=[
            pltpu.VMEM(((nx + 2 * reach) * ROWS, LANES), jnp.float32),
            pltpu.VMEM((zb * ny, LANES), jnp.float32),
        ],
        cost_estimate=COST,
        compiler_params=PARAMS,
    )(stack))
    late_perm, _ = lax.optimization_barrier((perm, packed[1]))
    length = max(extent, halo * tiles)

    bulk = lax.axis_index("bulk")
    even = bulk % 2 == 0

    def beside(first):
        planes = lax.dynamic_slice_in_dim(stack, first, halo, 0).reshape(halo, tiles, LANES)
        planes = jnp.swapaxes(planes, 0, 1).reshape(halo * tiles, LANES)
        return jnp.pad(planes, ((0, length - halo * tiles), (0, 0)))

    for k in neighbours(count):
        block = jnp.pad(packed[k], ((0, length - extent), (0, 0)))
        above = even if k == 1 else jnp.logical_not(even)
        start = jnp.where(above, (zb - reach) * ny, 0)
        packed[k] = jnp.where(late_perm[0] == 1, block, beside(start))
    packed[1], _ = lax.optimization_barrier((packed[1], packed[2]))
    blocks = {0: packed[0]}
    for k in range(count - 1, 0, -1):
        blocks[k] = lax.ppermute(packed[k], "bulk", [(i, i ^ k) for i in range(count)])
    blocks = [blocks[k] for k in range(count)]

    joined_taps = jnp.where(late_perm[0] == 1, kernels[::-1], kernels)
    scalars = jnp.stack([shift[0], core.astype(jnp.int32), late_perm[0]])

    swap = [(i, i ^ 1) for i in range(views)]
    def beside_of(v, i):
        there = i ^ 1 if v % 2 == 0 else ((i + 1) ^ 1) - 1
        return there if 0 <= there < count else i

    side = chip % 2
    start = jnp.where(even == (core == 0), zb - 2 * reach, 0) + reach * side
    quarter = lax.ppermute(
        lax.dynamic_slice_in_dim(estimate, start, reach, 0),
        ("view", "bulk"),
        [(v * count + i, v * count + beside_of(v, i)) for v in range(views) for i in range(count)],
    )
    across = lax.ppermute(quarter, "view", [(v, v ^ 2) for v in range(views)])
    near = jnp.concatenate([
        jnp.where(side == 0, quarter, across), jnp.where(side == 0, across, quarter)
    ])
    other = lax.ppermute(near, "view", swap)

    group = WIDE // ny
    planes = -(-(zb + 2 * reach) // group) * group
    inverse, rows_high, rows_low, lanes_pair, weight, splats, flags = pl.pallas_call(
        functools.partial(forward_kernel, zb, ny, nx, planes),
        out_shape=[
            struct((planes, ny, nx)),
            struct((WIDE, WIDE), jnp.bfloat16),
            struct((WIDE, WIDE), jnp.bfloat16),
            struct((2 * nx, 2 * nx), jnp.bfloat16),
            struct((zb, ROWS, LANES)),
            struct((taps, ROWS, LANES)),
            struct((ROWS, LANES), jnp.int32),
        ],
        in_specs=[SMEM] * 3 + [VMEM] * 3,
        out_specs=[VMEM] * 7,
        scratch_shapes=[pltpu.VMEM((planes + 2 * reach, ny, nx), jnp.float32)],
        cost_estimate=COST,
        compiler_params=PARAMS,
    )(scalars, joined_taps, visible[0], estimate, near, other)

    parts = 2
    size = zb // (2 * parts)
    matrices = (rows_high, rows_low, lanes_pair)
    first = pl.pallas_call(
        functools.partial(ratio_kernel, zb, ny, nx, count),
        out_shape=[struct((size, ny, nx))] * 2 + [struct((zb + 2 * reach, ny, nx))],
        in_specs=[VMEM] * (8 + count),
        out_specs=[VMEM] * 3,
        scratch_shapes=[
            pltpu.VMEM((count, (zb + 2 * reach) * ROWS, LANES), jnp.float32),
        ],
        cost_estimate=COST,
        compiler_params=PARAMS,
    )(flags, weight, splats, stack, inverse, *matrices, *blocks)
    total = [first[1] + lax.ppermute(first[0], "view", swap)]
    for part in range(1, parts):
        held = weight
        send, keep = pl.pallas_call(
            functools.partial(adjoint_kernel, part),
            out_shape=[struct((size, ny, nx))] * 2,
            in_specs=[VMEM] * 6,
            out_specs=[VMEM] * 2,
            cost_estimate=COST,
        compiler_params=PARAMS,
        )(held, splats, first[2], *matrices)
        total.append(keep + lax.ppermute(send, "view", swap))

    bits = (views // 2).bit_length() - 1
    result = []
    for part in range(parts):
        for step in range(bits):
            flips = [2 << step, 2 << ((step + bits - 1) % bits)]
            total[part] = total[part] + lax.ppermute(
                total[part], "view", [(i, i ^ flips[i % 2]) for i in range(views)]
            )
        held = estimate if not part else lax.optimization_barrier((estimate, own))[0]
        own = lax.dynamic_slice_in_dim(held, (2 * part + core) * size, size, 0)
        own = own * jnp.exp(total[part] / float(views))
        their = lax.ppermute(own, "view", swap)
        result += [jnp.where(core == 0, own, their), jnp.where(core == 0, their, own)]
    return jnp.concatenate(result, axis=0)


def solution(mesh):
    placed = (
        P("bulk", None, None),
        P("view", "bulk", None, None),
        P("view", None, None),
        P("view"),
        P("view"),
        P("view", "bulk"),
    )
    return jax.shard_map(
        shards, mesh=mesh, in_specs=placed, out_specs=P("bulk", None, None), check_vma=False
    )
```

```python
import functools

import jax
import jax.numpy as jnp
from jax import lax
from jax.experimental import pallas as pl
from jax.experimental.pallas import tpu as pltpu
from jax.sharding import PartitionSpec as P

LANES = 128
ROWS = 8
WIDE = 256
VMEM = pl.BlockSpec(memory_space=pltpu.VMEM)
SMEM = pl.BlockSpec(memory_space=pltpu.SMEM)
COST = pl.CostEstimate(flops=2**29, bytes_accessed=2**21, transcendentals=2**16)
PARAMS = pltpu.CompilerParams(vmem_limit_bytes=40 * 1024 * 1024)


def struct(shape, dtype=jnp.float32):
    return jax.ShapeDtypeStruct(shape, dtype)


def halves(values):
    high = values.astype(jnp.bfloat16)
    low = (values - high.astype(jnp.float32)).astype(jnp.bfloat16)
    return high, low


def dot(left, right):
    return jnp.dot(left, right, preferred_element_type=jnp.float32)


def blur_rows(left_high, left_low, values):
    width = values.shape[1]
    high, low = halves(values)
    both = dot(left_high, jnp.concatenate([high, low], axis=1))
    return both[:, :width] + both[:, width:] + dot(left_low, high)


def blur_lanes(right, values):
    width = values.shape[1]
    out = dot(jnp.concatenate(halves(values), axis=1), right)
    return out[:, :width] + out[:, width:]


def lanes_matrix(taps_ref, row, extent, adjoint):
    taps = taps_ref.shape[1]
    source = lax.broadcasted_iota(jnp.int32, (extent, extent), 0)
    target = lax.broadcasted_iota(jnp.int32, (extent, extent), 1)
    offset = (target - source if adjoint else source - target) + taps // 2
    matrix = jnp.zeros((extent, extent), jnp.float32)
    for t in range(taps):
        matrix = jnp.where(offset == t, taps_ref[row, t], matrix)
    high, low = halves(matrix)
    pair = jnp.concatenate([high, low], axis=1)
    return jnp.concatenate([pair, pair], axis=0)


def rows_matrix(taps_ref, row, period, moved, adjoint):
    taps = taps_ref.shape[1]
    target = lax.broadcasted_iota(jnp.int32, (period, WIDE), 0)
    source = lax.broadcasted_iota(jnp.int32, (period, WIDE), 1)
    ahead = target - source if adjoint else source - target
    offset = jnp.bitwise_and(ahead + taps // 2 + moved, period - 1)
    block = jnp.zeros((period, WIDE), jnp.float32)
    for t in range(taps):
        block = jnp.where(offset == t, taps_ref[row, t], block)
    plane = source // period
    return halves(
        jnp.concatenate([jnp.where(plane == p, block, 0.0) for p in range(WIDE // period)], axis=0)
    )


def blur_planes(source_ref, splats, base, group):
    ny, nx = source_ref.shape[1:]
    taps = len(splats)
    columns = []
    for tile in range(nx // LANES):
        lanes = slice(tile * LANES, (tile + 1) * LANES)
        places = []
        for row in range(ny // ROWS):
            rows = slice(row * ROWS, (row + 1) * ROWS)
            source = [source_ref[base + i, rows, lanes] for i in range(group + taps - 1)]
            sums = []
            for plane in range(group):
                total = splats[0] * source[plane]
                for t in range(1, taps):
                    total = total + splats[t] * source[plane + t]
                sums.append(total)
            places.append(sums)
        columns.append(
            jnp.concatenate([sums[plane] for plane in range(group) for sums in places], axis=0)
        )
    return columns[0] if len(columns) == 1 else jnp.concatenate(columns, axis=1)


def pack_kernel(zb, ny, nx, count, image_ref, *refs):
    sends, (turned_ref, tile_ref) = refs[:count], refs[count:]
    reach = 7
    b = lax.axis_index("bulk")
    groups = ny // ROWS
    extent = (zb + 2 * reach) * ROWS
    edge = jnp.zeros((reach * ROWS, LANES), jnp.float32)
    turned_ref[: reach * ROWS] = edge
    turned_ref[(reach + nx) * ROWS :] = edge
    for tile in range(nx // LANES):
        if nx > LANES:
            tile_ref[...] = image_ref[:, tile * LANES : (tile + 1) * LANES]
            source = tile_ref
        else:
            source = image_ref
        for low in range(ROWS):
            pieces = [
                source[pl.ds(ROWS * group + low, zb, stride=ny), :] for group in range(groups)
            ]
            block = jnp.concatenate(pieces, axis=0).T
            turned_ref[pl.ds((tile * LANES + reach) * ROWS + low, LANES, stride=ROWS), :] = block
    for k in range(count):
        start = jnp.bitwise_xor(b, k) * (zb * ROWS)
        sends[k][...] = turned_ref[pl.ds(pl.multiple_of(start, ROWS), extent), :]


def forward_kernel(zb, ny, nx, planes, scalar_ref, taps_ref, visible_ref, estimate_ref, near_ref,
                   other_ref, inverse_ref, rows_high_ref, rows_low_ref, lanes_ref,
                   weight_ref, splat_ref, flag_ref,
                   wide_ref):
    taps = taps_ref.shape[1]
    reach = taps // 2
    moved, core = scalar_ref[0], scalar_ref[1]
    flag_ref[...] = jnp.full((ROWS, LANES), scalar_ref[2], jnp.int32)
    wide_ref[2 * reach : 2 * reach + zb] = estimate_ref[...]
    b, count = lax.axis_index("bulk"), lax.axis_size("bulk")
    above = jnp.bitwise_xor(lax.rem(b, 2), 1 - core)
    for block_ref, side in ((near_ref, above), (other_ref, 1 - above)):
        inside = jnp.logical_and(b + 2 * side - 1 >= 0, b + 2 * side - 1 < count)
        wide_ref[pl.ds((2 * reach + zb) * side, 2 * reach)] = jnp.where(inside, block_ref[...], 0.0)
    rest = planes - zb - 2 * reach
    wide_ref[4 * reach + zb :] = jnp.zeros((rest, ny, nx), jnp.float32)

    rows_high, rows_low = rows_matrix(taps_ref, 1, ny, moved, False)
    lanes = lanes_matrix(taps_ref, 2, nx, False)
    group = WIDE // ny

    tile = (ROWS, LANES)
    splats = [jnp.full(tile, taps_ref[0, t], jnp.float32) for t in range(taps)]
    for t in range(taps):
        splat_ref[taps - 1 - t] = splats[t]
    for base in range(0, planes, group):
        values = blur_planes(wide_ref, splats, base, group)
        values = blur_lanes(lanes, blur_rows(rows_high, rows_low, values))
        inverse_ref[base : base + group] = (1.0 / values).reshape(group, ny, nx)
    high, low = rows_matrix(taps_ref, 1, ny, moved, True)
    rows_high_ref[...] = high
    rows_low_ref[...] = low
    lanes_ref[...] = lanes_matrix(taps_ref, 2, nx, True)
    for plane in range(zb):
        weight = jnp.where(visible_ref[plane] == 1, 1.0, 0.0)
        weight_ref[plane] = jnp.full((ROWS, LANES), weight, jnp.float32)


def neighbours(count):
    return [k for k in range(1, count) if k & (k + 1) == 0]


def beside_in(b, k):
    low = jnp.bitwise_and(b, k)
    return jnp.logical_or(low == k // 2, low == k // 2 + 1)


def ratio_kernel(zb, ny, nx, count, flag_ref, weight_ref, splat_ref, image_ref, inverse_ref,
                 rows_high_ref, rows_low_ref, lanes_ref, *refs):
    blocks, (send_ref, keep_ref, ratio_ref, placed_ref) = refs[:count], refs[count:]
    reach = splat_ref.shape[0] // 2
    b = lax.axis_index("bulk")
    groups = ny // ROWS
    planes = zb + 2 * reach
    turned = flag_ref[...] == 1
    for k in range(count):
        placed_ref[jnp.bitwise_xor(b, k)] = blocks[k][: planes * ROWS]
    odd = lax.rem(b, 2) == 1
    spot = lax.broadcasted_iota(jnp.int32, (ROWS, LANES), 1) // zb
    outside = {0: b > 0, reach + zb: b < count - 1}
    for tile in range(nx // LANES):
        lanes = slice(tile * LANES, (tile + 1) * LANES)
        for plane in range(planes):
            place = slice(plane * ROWS, (plane + 1) * ROWS)
            pieces = [placed_ref[groups * tile + c, place] for c in range(groups)]
            for g in range(groups):
                rows = slice(g * ROWS, (g + 1) * ROWS)
                value = None
                for c in range(groups):
                    shift = (zb * (c - g)) % LANES
                    moved = pltpu.roll(pieces[c], shift, 1) if shift else pieces[c]
                    value = moved if value is None else jnp.where(spot == c, moved, value)
                if reach <= plane < reach + zb:
                    start = (plane - reach) * ny + g * ROWS
                    straight = image_ref[start : start + ROWS, lanes]
                else:
                    side = 0 if plane < reach else reach + zb
                    start = (tile * reach + plane - side) * ny + g * ROWS
                    beside = [blocks[k][start : start + ROWS] for k in neighbours(count)]
                    far = beside[1]
                    for k, value2 in zip(neighbours(count)[2:], beside[2:]):
                        far = jnp.where(beside_in(b, k), value2, far)
                    straight = jnp.where(odd == (side == 0), beside[0], far)
                    straight = jnp.where(outside[side], straight, 0.0)
                value = jnp.where(turned, value, straight)
                ratio_ref[plane, rows, lanes] = value * inverse_ref[plane, rows, lanes]

    adjoint_kernel(0, weight_ref, splat_ref, ratio_ref, rows_high_ref, rows_low_ref, lanes_ref,
                   send_ref, keep_ref)


def adjoint_kernel(part, weight_ref, splat_ref, ratio_ref, rows_high_ref, rows_low_ref, lanes_ref,
                   send_ref, keep_ref):
    core = lax.rem(lax.axis_index("view"), 2)
    splats = [splat_ref[t] for t in range(splat_ref.shape[0])]
    rows_high, rows_low, lanes_pair = rows_high_ref[...], rows_low_ref[...], lanes_ref[...]
    size, ny, nx = send_ref.shape
    group = WIDE // ny
    for out_ref, side in ((send_ref, 1 - core), (keep_ref, core)):
        for first in range(0, size, group):
            base = (2 * part + side) * size + first
            values = blur_planes(ratio_ref, splats, base, group)
            values = blur_lanes(lanes_pair, blur_rows(rows_high, rows_low, values))
            logs = jnp.log(values).reshape(group, ny // ROWS, ROWS, nx)
            for plane in range(group):
                weight = weight_ref[base + plane]
                for tile in range(nx // LANES):
                    lanes = slice(tile * LANES, (tile + 1) * LANES)
                    for row in range(ny // ROWS):
                        out_ref[first + plane, row * ROWS : (row + 1) * ROWS, lanes] = (
                            weight * logs[plane, row, :, lanes]
                        )


def shards(estimate, image, psf, perm, shift, visible):
    zb, ny, nx = estimate.shape
    views, count = lax.axis_size("view"), lax.axis_size("bulk")
    view = lax.axis_index("view")
    core, chip = view % 2, view // 2
    taps = psf.shape[2]
    reach = taps // 2
    kernels = psf[0] / jnp.sum(psf[0], axis=1, keepdims=True)
    stack = image[0].reshape(zb * ny, nx)

    tiles = nx // LANES
    halo = reach * ny
    extent = (zb + 2 * reach) * ROWS
    packed = list(pl.pallas_call(
        functools.partial(pack_kernel, zb, ny, nx, count),
        out_shape=[struct((extent, LANES))] * count,
        in_specs=[VMEM],
        out_specs=[VMEM] * count,
        scratch_shapes=[
            pltpu.VMEM(((nx + 2 * reach) * ROWS, LANES), jnp.float32),
            pltpu.VMEM((zb * ny, LANES), jnp.float32),
        ],
        compiler_params=PARAMS,
    )(stack))
    late_perm, _ = lax.optimization_barrier((perm, packed[1]))
    length = max(extent, halo * tiles)

    bulk = lax.axis_index("bulk")
    even = bulk % 2 == 0

    def beside(first):
        planes = lax.dynamic_slice_in_dim(stack, first, halo, 0).reshape(halo, tiles, LANES)
        planes = jnp.swapaxes(planes, 0, 1).reshape(halo * tiles, LANES)
        return jnp.pad(planes, ((0, length - halo * tiles), (0, 0)))

    for k in neighbours(count):
        block = jnp.pad(packed[k], ((0, length - extent), (0, 0)))
        above = even if k == 1 else jnp.logical_not(even)
        start = jnp.where(above, (zb - reach) * ny, 0)
        packed[k] = jnp.where(late_perm[0] == 1, block, beside(start))
    packed[1], _ = lax.optimization_barrier((packed[1], packed[2]))
    blocks = {0: packed[0]}
    for k in range(count - 1, 0, -1):
        blocks[k] = lax.ppermute(packed[k], "bulk", [(i, i ^ k) for i in range(count)])
    blocks = [blocks[k] for k in range(count)]

    joined_taps = jnp.where(late_perm[0] == 1, kernels[::-1], kernels)
    scalars = jnp.stack([shift[0], core.astype(jnp.int32), late_perm[0]])

    swap = [(i, i ^ 1) for i in range(views)]
    def beside_of(v, i):
        there = i ^ 1 if v % 2 == 0 else ((i + 1) ^ 1) - 1
        return there if 0 <= there < count else i

    side = chip % 2
    start = jnp.where(even == (core == 0), zb - 2 * reach, 0) + reach * side
    quarter = lax.ppermute(
        lax.dynamic_slice_in_dim(estimate, start, reach, 0),
        ("view", "bulk"),
        [(v * count + i, v * count + beside_of(v, i)) for v in range(views) for i in range(count)],
    )
    across = lax.ppermute(quarter, "view", [(v, v ^ 2) for v in range(views)])
    near = jnp.concatenate([
        jnp.where(side == 0, quarter, across), jnp.where(side == 0, across, quarter)
    ])
    other = lax.ppermute(near, "view", swap)

    group = WIDE // ny
    planes = -(-(zb + 2 * reach) // group) * group
    inverse, rows_high, rows_low, lanes_pair, weight, splats, flags = pl.pallas_call(
        functools.partial(forward_kernel, zb, ny, nx, planes),
        out_shape=[
            struct((planes, ny, nx)),
            struct((WIDE, WIDE), jnp.bfloat16),
            struct((WIDE, WIDE), jnp.bfloat16),
            struct((2 * nx, 2 * nx), jnp.bfloat16),
            struct((zb, ROWS, LANES)),
            struct((taps, ROWS, LANES)),
            struct((ROWS, LANES), jnp.int32),
        ],
        in_specs=[SMEM] * 3 + [VMEM] * 3,
        out_specs=[VMEM] * 7,
        scratch_shapes=[pltpu.VMEM((planes + 2 * reach, ny, nx), jnp.float32)],
        compiler_params=PARAMS,
    )(scalars, joined_taps, visible[0], estimate, near, other)

    parts = 2
    size = zb // (2 * parts)
    matrices = (rows_high, rows_low, lanes_pair)
    first = pl.pallas_call(
        functools.partial(ratio_kernel, zb, ny, nx, count),
        out_shape=[struct((size, ny, nx))] * 2 + [struct((zb + 2 * reach, ny, nx))],
        in_specs=[VMEM] * (8 + count),
        out_specs=[VMEM] * 3,
        scratch_shapes=[
            pltpu.VMEM((count, (zb + 2 * reach) * ROWS, LANES), jnp.float32),
        ],
        compiler_params=PARAMS,
    )(flags, weight, splats, stack, inverse, *matrices, *blocks)
    total = [first[1] + lax.ppermute(first[0], "view", swap)]
    for part in range(1, parts):
        held = weight
        send, keep = pl.pallas_call(
            functools.partial(adjoint_kernel, part),
            out_shape=[struct((size, ny, nx))] * 2,
            in_specs=[VMEM] * 6,
            out_specs=[VMEM] * 2,
            cost_estimate=COST,
            compiler_params=PARAMS,
        )(held, splats, first[2], *matrices)
        total.append(keep + lax.ppermute(send, "view", swap))

    bits = (views // 2).bit_length() - 1
    result = []
    for part in range(parts):
        for step in range(bits):
            flips = [2 << ((step + bits - 1) % bits), 2 << step]
            total[part] = total[part] + lax.ppermute(
                total[part], "view", [(i, i ^ flips[i % 2]) for i in range(views)]
            )
        held = estimate if not part else lax.optimization_barrier((estimate, own))[0]
        own = lax.dynamic_slice_in_dim(held, (2 * part + core) * size, size, 0)
        own = own * jnp.exp(total[part] / float(views))
        their = lax.ppermute(own, "view", swap)
        result += [jnp.where(core == 0, own, their), jnp.where(core == 0, their, own)]
    return jnp.concatenate(result, axis=0)


def solution(mesh):
    placed = (
        P("bulk", None, None),
        P("view", "bulk", None, None),
        P("view", None, None),
        P("view"),
        P("view"),
        P("view", "bulk"),
    )
    return jax.shard_map(
        shards, mesh=mesh, in_specs=placed, out_specs=P("bulk", None, None), check_vma=False
    )
```
